512 devices in a mesh: seq: 64 (over x, z), head: 8 (over y, core).
Axes of the slice: x: 4, y: 4, z: 16, core: 2. Of those that a mesh axis runs over, the one named last changes fastest.
Arguments:
- queries: bfloat16 [24576, 4096], P(('seq', 'head')), may hold values from -5 to 5
- keys: bfloat16 [24576, 4096], P(('seq', 'head')), may hold values from -5 to 5
- values: bfloat16 [24576, 4096], P(('seq', 'head')), may hold values from -6 to 6
- dout: bfloat16 [24576, 4096], P(('seq', 'head')), may hold values from -6 to 6
- selected: int32 [1024, 3], P('seq'), may hold values from 0 to 63, as said below
Outputs:
- attended: bfloat16 [24576, 4096], P('seq', 'head')
- grad_queries: bfloat16 [24576, 4096], P('seq', 'head')
- grad_keys: bfloat16 [24576, 4096], P('seq', 'head')
- grad_values: bfloat16 [24576, 4096], P('seq', 'head')
The draws below stay inside these ranges and needn't reach their ends.
Inputs may be any that keep to these rules, and one draw needn't show every extreme that they name: `selected`: row g belongs to query block g in key-value block b = g // 16; an entry equal to b marks an unused slot, the other entries of a row are distinct and smaller than b; among the 16 rows of one key-value block no other block is named more than 1 times.
All inputs are finite; a program needn't handle non-finite values.
Results may differ from the reference program's by a relative error of at most 0.014.
The reference program's roundings to bfloat16 on the way count: a program that leaves them out, or rounds other values in their place, can miss the bound.
Values may be sent and summed in bfloat16 or wider, within the bound.
A program may use at most 64 MiB of HBM per device.

```python
import math
import jax
import jax.numpy as jnp
from jax import lax

HD = 128
TOK_DEV = 384
QB = 24
TOPK = 3
CAP = 1
HEADS = 32
TOKENS = 24576
NQB = 1024
N_SEQ = 64


def draw_queries(key, part):
    key = jax.random.fold_in(key, 21)
    result = jnp.clip(jax.random.normal(key, (TOKENS, HEADS * HD), jnp.float32), -5.0, 5.0)
    return result.astype(jnp.bfloat16)


def draw_keys(key, part):
    key = jax.random.fold_in(key, 22)
    result = jnp.clip(jax.random.normal(key, (TOKENS, HEADS * HD), jnp.float32), -5.0, 5.0)
    return result.astype(jnp.bfloat16)


def draw_selected(key, part):
    key = jax.random.fold_in(key, 23)
    block_count = TOK_DEV // QB
    blocks = TOKENS // TOK_DEV
    owner_ids = jnp.arange(blocks, dtype=jnp.int32)
    scores = jax.random.randint(key, (blocks, blocks), 0, 1 << 20, dtype=jnp.int32) * blocks + owner_ids[None, :]
    scores = jnp.where(owner_ids[None, :] < owner_ids[:, None], scores, (1 << 30) + owner_ids[None, :])
    ordering = jnp.argsort(scores, axis=1)
    query_line = jnp.arange(NQB, dtype=jnp.int32)
    device = query_line // block_count
    within = query_line % block_count
    slot_ids = jnp.arange(TOPK, dtype=jnp.int32)
    counter = TOPK * within[:, None] + slot_ids[None, :]
    earlier = device[:, None]
    usable = (counter < CAP * earlier) & (slot_ids[None, :] < earlier)
    final_slot = (device[:, None] == blocks - 1) & (within[:, None] == block_count - 1) & (slot_ids[None, :] == TOPK - 1)
    usable = usable & jnp.logical_not(final_slot)
    picked = ordering[device[:, None], counter % jnp.maximum(earlier, 1)]
    return jnp.where(usable, picked, earlier).astype(jnp.int32)


def shard_levels(rng, extent, pieces, smallest, high):
    gain, own = 1.0, jax.random.fold_in(rng, 6)
    for dim, blocks in pieces:
        heights = jnp.exp(jax.random.uniform(jax.random.fold_in(own, dim), (blocks,), jnp.float32, smallest / len(pieces), high / len(pieces)))
        gain = gain * jnp.repeat(heights, extent[dim] // blocks).reshape([-1 if axis == dim else 1 for axis in range(len(extent))])
    return gain


def centred(rng, dims, spread, reach, shards=(), held_as=jnp.bfloat16):
    level = shard_levels(rng, dims, shards, -0.22, 0.18) if shards else 1.0
    values = jax.random.normal(rng, dims, jnp.float32) * spread * level
    return jnp.minimum(jnp.maximum(values, -reach), reach).astype(held_as)


def setup_inputs(seed: int = 0) -> dict:
    arg_keys = jax.random.split(jax.random.key(seed), 6)
    return {
        "queries": draw_queries(jax.random.fold_in(arg_keys[5], 71), 0),
        "keys": draw_keys(jax.random.fold_in(arg_keys[5], 71), 0),
        "values": centred(arg_keys[2], (TOKENS, HEADS * HD), 1.0, 6.0, ((0, 512),)),
        "dout": centred(arg_keys[3], (TOKENS, HEADS * HD), 1.0, 6.0, ((0, 512),)),
        "selected": draw_selected(jax.random.fold_in(arg_keys[5], 71), 0),
    }


NEGATIVE = -1e+30

def rounded(value):
    return lax.optimization_barrier(value.astype(jnp.bfloat16)).astype(jnp.float32)

def reference(queries, keys, values, dout, selected):
    scale = 1.0 / math.sqrt(HD)
    block_count = TOK_DEV // QB
    chosen_all = selected.reshape(N_SEQ, block_count, TOPK)
    positions = jnp.arange(TOK_DEV, dtype=jnp.int32)
    causal = (positions[:, None] >= positions[None, :]).reshape(block_count, QB, TOK_DEV)

    def by_head(array):
        return array.reshape(N_SEQ, TOK_DEV, HEADS, HD).transpose(2, 0, 1, 3)

    def per_head(inputs):
        q_head, k_head, v_head, g_head = inputs

        def per_device(carry, device):
            grad_k, grad_v = carry
            query = q_head[device].astype(jnp.float32).reshape(block_count, QB, HD)
            upstream = g_head[device].astype(jnp.float32).reshape(block_count, QB, HD)
            chosen = chosen_all[device]
            active = chosen != device
            far_keys = k_head[chosen].astype(jnp.float32)
            far_values = v_head[chosen].astype(jnp.float32)
            own_keys = k_head[device].astype(jnp.float32)
            own_values = v_head[device].astype(jnp.float32)
            far_scores = jnp.einsum('gqd,gskd->gsqk', query, far_keys) * scale
            far_peak = lax.optimization_barrier(jnp.max(far_scores, axis=3, keepdims=True))
            far_lse = far_peak + jnp.log(lax.optimization_barrier(jnp.sum(jnp.exp(far_scores - far_peak), axis=3, keepdims=True)))
            far_out = rounded(jnp.einsum('gsqk,gskd->gsqd', rounded(jnp.exp(far_scores - far_lse)), far_values))
            far_lse = jnp.where(active[:, :, None], far_lse[..., 0], NEGATIVE)
            own_scores = jnp.where(causal, jnp.einsum('gqd,kd->gqk', query, own_keys) * scale, NEGATIVE)
            own_peak = lax.optimization_barrier(jnp.max(own_scores, axis=2, keepdims=True))
            own_lse = own_peak + jnp.log(lax.optimization_barrier(jnp.sum(jnp.exp(own_scores - own_peak), axis=2, keepdims=True)))
            own_out = rounded(jnp.einsum('gqk,kd->gqd', rounded(jnp.exp(own_scores - own_lse)), own_values))
            all_lse = jnp.concatenate([own_lse[:, None, :, 0], far_lse], axis=1)
            all_out = jnp.concatenate([own_out[:, None], far_out], axis=1)
            lse_peak = lax.optimization_barrier(jnp.max(all_lse, axis=1, keepdims=True))
            log_total = lse_peak + jnp.log(lax.optimization_barrier(jnp.sum(jnp.exp(all_lse - lse_peak), axis=1, keepdims=True)))
            weights = jnp.exp(all_lse - log_total)
            attended = rounded(lax.optimization_barrier(jnp.sum(weights[..., None] * all_out, axis=1)))
            delta = lax.optimization_barrier(jnp.sum(upstream * attended, axis=2))
            far_probs = jnp.where(active[:, :, None, None], jnp.exp(far_scores - log_total[:, :, :, None]), 0.0)
            far_dv = jnp.einsum('gsqk,gqd->gskd', rounded(far_probs), upstream)
            far_ds = rounded(far_probs * (jnp.einsum('gqd,gskd->gsqk', upstream, far_values) - delta[:, None, :, None]))
            far_dq = rounded(jnp.einsum('gsqk,gskd->gsqd', far_ds, far_keys) * scale)
            far_dk = jnp.einsum('gsqk,gqd->gskd', far_ds, query) * scale
            own_probs = jnp.exp(own_scores - log_total[:, 0, :, None])
            own_dv = jnp.einsum('gqk,gqd->kd', rounded(own_probs), upstream)
            own_ds = rounded(own_probs * (jnp.einsum('gqd,kd->gqk', upstream, own_values) - delta[:, :, None]))
            own_dq = rounded(jnp.einsum('gqk,kd->gqd', own_ds, own_keys) * scale)
            own_dk = jnp.einsum('gqk,gqd->kd', own_ds, query) * scale
            grad_q = own_dq + lax.optimization_barrier(jnp.sum(far_dq, axis=1))
            flat_chosen = chosen.reshape(-1)
            grad_k = grad_k.at[flat_chosen].add(far_dk.reshape(-1, TOK_DEV, HD)).at[device].add(own_dk)
            grad_v = grad_v.at[flat_chosen].add(far_dv.reshape(-1, TOK_DEV, HD)).at[device].add(own_dv)
            return ((grad_k, grad_v), (attended.reshape(TOK_DEV, HD), grad_q.reshape(TOK_DEV, HD)))
        start = jnp.zeros((N_SEQ, TOK_DEV, HD), jnp.float32)
        (grad_k, grad_v), (attended, grad_q) = lax.scan(per_device, (start, start), jnp.arange(N_SEQ, dtype=jnp.int32))
        return (attended, grad_q, grad_k, grad_v)
    results = lax.map(per_head, (by_head(queries), by_head(keys), by_head(values), by_head(dout)))

    def unhead(array):
        return array.transpose(1, 2, 0, 3).reshape(TOKENS, HEADS * HD).astype(jnp.bfloat16)
    return (unhead(results[0]), unhead(results[1]), unhead(results[2]), unhead(results[3]))
```

```python
import functools
import math

import jax
import jax.numpy as jnp
import numpy as np
from jax import lax
from jax.experimental import pallas as pl
from jax.experimental.pallas import tpu as pltpu
from jax.sharding import PartitionSpec as P

HD = 128
QB = 24
TOPK = 3
ZN = 16
NEGATIVE = -1e30
MESH = pl.DeviceIdType.MESH
BF = jnp.bfloat16
F32 = jnp.float32
VMEM_LIMIT = 60 * 1024 * 1024


def dot(a, b, ca, cb):
    return lax.dot_general(a, b, (((ca,), (cb,)), ((), ())), preferred_element_type=F32)


def split3(a):
    high = a.astype(BF)
    rest = a - high.astype(F32)
    mid = rest.astype(BF)
    low = (rest - mid.astype(F32)).astype(BF)
    return jnp.concatenate([high, mid, low], axis=0)


def loop(start, stop, body):
    def step(index, carry):
        body(index)
        return carry

    lax.fori_loop(start, stop, step, 0)


def kernel(
    xn, zn, hn, heads,
    sel, inv, flag, spread, owner_mask, q_in, k_in, v_in, g_in,
    att, gq, gk, gv,
    qa, ka, va, ga, qf, gf, kh, vh, kt, vt,
    pk, r1, f, rt, r2, g0, g1, g2, g3, su, srx, s0, s1, ws, wrz, wr,
    qc, gc, pb, db, li, sv, wv, dk, dv, aj, lr, dr, fo,
    ssem, rsem, lsem,
):
    scale = 1.0 / math.sqrt(HD)
    seq = lax.axis_index("seq")
    head = lax.axis_index("head")
    x = lax.div(seq, zn)
    z = lax.rem(seq, zn)
    rows = q_in.shape[0]
    width = heads * HD
    tokens = qa.shape[0]
    far = zn * QB

    def z_partner(k):
        half = lax.div(k + 1, 2)
        return lax.rem(z + jnp.where(lax.rem(k, 2) == 1, half, zn - half), zn)

    def z_send(src, dst, lower, down, flow):
        def body(k):
            zi = z_partner(k)
            own = jnp.where(zi < z, 1, 0) if down else jnp.where(zi > z, 1, 0)
            start = 0 if lower else x + 1 - own
            count = x + own if lower else xn - 1 - x + own
            for m in range(1, xn + 1):

                @pl.when(count == m)
                def _():
                    pltpu.make_async_remote_copy(
                        src_ref=src.at[pl.ds(start, m), zi],
                        dst_ref=dst.at[pl.ds(start, m), z],
                        send_sem=ssem.at[flow, zi],
                        recv_sem=rsem.at[flow, z],
                        device_id={"seq": x * zn + zi},
                        device_id_type=MESH,
                    ).start()

        loop(1, zn, body)

    def z_wait(buf, lower, down, sem, sent):
        base = x if lower else xn - 1 - x

        def body(k):
            zi = z_partner(k)
            below = jnp.where(zi < z, 1, 0)
            count = base + (below if down == sent else 1 - below)
            for m in range(1, xn + 1):

                @pl.when(count == m)
                def _():
                    part = buf.at[0, pl.ds(0, m)]
                    pltpu.make_async_copy(part, part, sem.at[zi]).wait()

        loop(1, zn, body)

    def x_send(src, dst, down, flow):
        def body(xi):
            pltpu.make_async_remote_copy(
                src_ref=src.at[xi],
                dst_ref=dst.at[x],
                send_sem=ssem.at[flow, xi],
                recv_sem=rsem.at[flow, x],
                device_id={"seq": xi * zn + z},
                device_id_type=MESH,
            ).start()

        if down:
            loop(0, x, body)
        else:
            loop(x + 1, xn, body)

    def x_wait(buf, down, sem, sent):
        whole = buf.at[0]
        body = lambda xi: pltpu.make_async_copy(whole, whole, sem.at[xi]).wait()
        if down == sent:
            loop(0, x, body)
        else:
            loop(x + 1, xn, body)

    def keep(dst, src, index):
        dst[index] = src[index]

    def down_first(src, mid, zf, flow):
        if zf:
            loop(0, xn, lambda i: keep(mid, src, (i, z)))
            z_send(src, mid, True, True, flow)
        else:
            loop(0, zn, lambda i: keep(mid, src, (x, i)))
            x_send(src, mid, True, flow)

    def down_second(mid, dst, zf, flow):
        if zf:
            z_wait(mid, True, True, rsem.at[flow], False)
            x_send(mid, dst, True, flow + 1)
        else:
            x_wait(mid, True, rsem.at[flow], False)
            z_send(mid, dst, False, True, flow + 1)

    def down_done(mid, dst, zf, flow):
        if zf:
            loop(z + 1, zn, lambda i: keep(dst, mid, (x, i)))
            x_wait(dst, True, rsem.at[flow + 1], False)
        else:
            loop(x + 1, xn, lambda i: keep(dst, mid, (i, z)))
            z_wait(dst, False, True, rsem.at[flow + 1], False)

    def up_first(src, mid, zf, flow):
        if zf:
            loop(0, zn, lambda i: keep(mid, src, (x, i)))
            x_send(src, mid, False, flow)
        else:
            loop(x + 1, xn, lambda i: keep(mid, src, (i, z)))
            z_send(src, mid, False, False, flow)

    def up_second(mid, dst, zf, flow):
        if zf:
            x_wait(mid, False, rsem.at[flow], False)
            z_send(mid, dst, True, False, flow + 1)
        else:
            z_wait(mid, False, False, rsem.at[flow], False)
            x_send(mid, dst, False, flow + 1)

    def up_done(mid, dst, zf, flow):
        if zf:
            loop(0, x, lambda i: keep(dst, mid, (i, z)))
            z_wait(dst, True, False, rsem.at[flow + 1], False)
        else:
            loop(0, z, lambda i: keep(dst, mid, (x, i)))
            x_wait(dst, False, rsem.at[flow + 1], False)

    def drain(buf, zf, flow, down):
        first_z = zf if down else not zf
        z_flow = flow if first_z else flow + 1
        x_flow = flow + 1 if first_z else flow
        z_wait(buf, zf, down, ssem.at[z_flow], True)
        x_wait(buf, down, ssem.at[x_flow], True)

    gg, sr = (g0, g1, g2, g3), (s0, s1)
    zfirst = [h % 2 == 0 for h in range(heads)]
    flow_down = [4 * h for h in range(heads)]
    flow_up = [4 * h + 2 for h in range(heads)]
    flow_stat = [4 * heads + 4 * s for s in range(heads // 2)]
    flow_head = 4 * heads + 4 * (heads // 2)

    f[...] = jnp.zeros_like(f)
    wr[...] = jnp.zeros_like(wr)
    for part in sr:
        part[...] = jnp.zeros_like(part)

    barrier = pltpu.get_barrier_semaphore()

    def greet(target):
        pl.semaphore_signal(barrier, inc=1, device_id=target, device_id_type=MESH)

    loop(1, hn, lambda i: greet({"head": lax.rem(head + i, hn)}))
    loop(1, zn, lambda i: greet({"seq": x * zn + lax.rem(z + i, zn)}))
    loop(1, xn, lambda i: greet({"seq": lax.rem(x + i, xn) * zn + z}))
    pl.semaphore_wait(barrier, hn + zn + xn - 3)

    inputs = ((q_in, qa), (g_in, ga), (k_in, ka), (v_in, va))
    here = pl.ds(pl.multiple_of(head * rows, rows), rows)

    for n, (src, dst) in enumerate(inputs):

        def fan(i, src=src, dst=dst, n=n):
            hi = lax.rem(head + i, hn)
            pltpu.make_async_remote_copy(
                src_ref=src.at[:, pl.ds(pl.multiple_of(hi * width, width), width)],
                dst_ref=dst.at[here],
                send_sem=ssem.at[flow_head + n, hi],
                recv_sem=rsem.at[flow_head + n, head],
                device_id={"head": hi},
                device_id_type=MESH,
            ).start()

        loop(1, hn, fan)
        pltpu.make_async_copy(
            src.at[:, pl.ds(pl.multiple_of(head * width, width), width)], dst.at[here], lsem.at[n]
        ).start()

    def head_wait(dst, sem):
        part = dst.at[pl.ds(0, rows)]

        def body(i):
            pltpu.make_async_copy(part, part, sem.at[lax.rem(head + i, hn)]).wait()

        loop(1, hn, body)

    def arrive(n):
        src, dst = inputs[n]
        pltpu.make_async_copy(
            src.at[:, pl.ds(pl.multiple_of(head * width, width), width)], dst.at[here], lsem.at[n]
        ).wait()
        head_wait(dst, rsem.at[flow_head + n])

    arrive(0)
    qf[...] = qa[...].astype(F32).reshape(qf.shape)
    arrive(1)
    gf[...] = ga[...].astype(F32).reshape(gf.shape)

    def block_of(i, h):
        cols = slice(h * HD, (h + 1) * HD)
        return jnp.concatenate([qf[i, :, cols], gf[i, :, cols]], axis=0).astype(BF)

    def pack(stage):
        def body(zd):
            for h in (2 * stage, 2 * stage + 1):
                f[h, xn, zd] = block_of(zd, h)
            for xd in range(xn):
                i = inv[xd * zn + zd]
                for h in (2 * stage, 2 * stage + 1):
                    pk[h, xd, zd] = block_of(i, h)

        loop(0, zn, body)
        for h in (2 * stage, 2 * stage + 1):
            down_first(pk.at[h], r1.at[h], zfirst[h], flow_down[h])

    def forward_relay(h):
        down_second(r1.at[h], f.at[h], zfirst[h], flow_down[h])

    def scores(stage):
        u = lax.broadcasted_iota(jnp.int32, (tokens, far), 0)
        t = lax.broadcasted_iota(jnp.int32, (tokens, far), 1)

        def body(step):
            hh = lax.rem(step, 2)
            group = x + lax.div(step, 2)
            h = 2 * stage + hh
            both = f[h, group].astype(F32)
            qv = both[:, :QB].reshape(far, HD).astype(BF)
            gv_ = both[:, QB:].reshape(far, HD).astype(BF)
            qc[hh, group] = qv
            gc[hh, group] = gv_
            s = dot(kh[h], qv, 1, 1)
            dp = dot(vh[h], gv_, 1, 1)
            s = jnp.where(u <= t + jnp.where(group == xn, 0, tokens), s, NEGATIVE)
            peak = jnp.max(s, axis=0, keepdims=True)
            p = jnp.exp((s - peak) * scale)
            total = jnp.sum(p, axis=0, keepdims=True)
            pb[hh, group] = p
            db[hh, group] = dp
            inverse = 1.0 / total
            li[hh, group] = inverse
            sv[group, hh] = peak * scale + jnp.log(total)
            sv[group, 2 + hh] = jnp.sum(p * dp, axis=0, keepdims=True) * inverse

        loop(0, 2 * (xn + 1 - x), body)

        def to_rows(group):
            mask = owner_mask[...]
            parts = split3(jnp.concatenate([sv[group, k] * mask for k in range(4)], axis=0))
            flat = dot(parts, spread[...], 1, 1)
            flat = flat[: 4 * zn] + flat[4 * zn : 8 * zn] + flat[8 * zn :]
            out = flat[:zn]
            for k in range(1, 4):
                out = out + pltpu.roll(flat[k * zn : (k + 1) * zn], QB * k, 1)
            for i in range(zn):
                su[stage, group, i] = out[i : i + 1]

        loop(x, xn + 1, to_rows)

    def combine(stage):
        lane = lax.broadcasted_iota(jnp.int32, (1, HD), 1)

        def gather(i):
            aj[0, pl.ds(i, 1)] = su[stage, xn, i]
            for j in range(TOPK):
                c = sel[i, j]
                row = sr[stage][lax.div(c, zn), lax.rem(c, zn)]
                aj[1 + j, pl.ds(i, 1)] = jnp.where(c == seq, NEGATIVE, row)

        loop(0, zn, gather)
        every = [aj[j] for j in range(TOPK + 1)]
        peak = functools.reduce(jnp.maximum, every)
        total = functools.reduce(jnp.add, [jnp.exp(a - peak) for a in every])
        lse = peak + jnp.log(total)
        weights = [jnp.exp(a - lse) for a in every]
        delta = functools.reduce(
            jnp.add, [pltpu.roll(w, 2 * QB, 1) * a for w, a in zip(weights, every)]
        )
        own = jnp.where(lane < 2 * QB, weights[0], delta)
        for i in range(zn):
            wr[stage, xn, i] = own[i : i + 1]
            lr[i] = lse[i : i + 1]
            dr[i] = delta[i : i + 1]

        def slots(xd):
            for zd in range(zn):
                c = xd * zn + zd
                i = inv[c]
                line = jnp.where(flag[c] > 0, lr[i], -NEGATIVE)
                w = jnp.exp(sr[stage][xd, zd] - line)
                ws[stage, xd, zd] = jnp.where(lane < 2 * QB, w, dr[i])

        loop(0, xn, slots)

    def exchange(stage):
        flow = flow_stat[stage]
        up_first(su.at[stage], srx.at[stage], True, flow + 2)
        up_second(srx.at[stage], sr[stage], True, flow + 2)
        up_done(srx.at[stage], sr[stage], True, flow + 2)
        combine(stage)
        down_first(ws.at[stage], wrz.at[stage], True, flow)
        down_second(wrz.at[stage], wr.at[stage], True, flow)
        down_done(wrz.at[stage], wr.at[stage], True, flow)

    def gradients(stage):
        def to_lanes(group):
            m = jnp.concatenate([wr[stage, group, i] for i in range(zn)], axis=0)
            wide = [m] + [pltpu.roll(m, HD - QB * k, 1) for k in range(1, 4)]
            flat = dot(split3(jnp.concatenate(wide, axis=0)), spread[...], 1, 0)
            flat = flat[: 4 * zn] + flat[4 * zn : 8 * zn] + flat[8 * zn :]
            mask = owner_mask[...]
            for k in range(4):
                wv[group, k] = jnp.sum(flat[k * zn : (k + 1) * zn] * mask, axis=0, keepdims=True)

        loop(x, xn + 1, to_lanes)

        def body(step):
            hh = lax.rem(step, 2)
            group = x + lax.div(step, 2)
            h = 2 * stage + hh
            p = pb[hh, group] * (wv[group, hh] * li[hh, group])
            pr = p.astype(BF)
            ds = (p * (db[hh, group] - wv[group, 2 + hh])).astype(BF)
            out = dot(vt[h], pr, 1, 0).T.reshape(zn, QB, HD)
            dq = (dot(kt[h], ds, 1, 0) * scale).T.reshape(zn, QB, HD)
            rt[h, group] = jnp.concatenate([out, dq], axis=1).astype(BF)
            dk[h] += dot(ds, qc[hh, group], 1, 0)
            dv[h] += dot(pr, gc[hh, group], 1, 0)

        loop(0, 2 * (xn + 1 - x), body)

    def finish(stage):
        for h in (2 * stage, 2 * stage + 1):

            def body(i, h=h):
                acc = rt[h, xn, i].astype(F32)
                for j in range(TOPK):
                    c = sel[i, j]
                    part = gg[h][lax.div(c, zn), lax.rem(c, zn)].astype(F32)
                    acc = acc + jnp.where(c == seq, 0.0, part)
                fo[i] = acc

            loop(0, zn, body)
            cols = slice(h * HD, (h + 1) * HD)
            att[:, cols] = fo[:, :QB].reshape(tokens, HD).astype(BF)
            gq[:, cols] = fo[:, QB:].reshape(tokens, HD).astype(BF)
            gk[:, cols] = (dk[h] * scale).astype(BF)
            gv[:, cols] = dv[h].astype(BF)

    pack(0)
    forward_relay(1)
    pack(1)
    arrive(2)
    arrive(3)
    for h in range(heads):
        cols = slice(h * HD, (h + 1) * HD)
        kh[h] = ka[:, cols]
        vh[h] = va[:, cols]
        kt[h] = ka[:, cols].T
        vt[h] = va[:, cols].T
    dk[...] = jnp.zeros_like(dk)
    dv[...] = jnp.zeros_like(dv)
    forward_relay(3)
    forward_relay(0)
    down_done(r1.at[0], f.at[0], zfirst[0], flow_down[0])
    down_done(r1.at[1], f.at[1], zfirst[1], flow_down[1])
    scores(0)
    exchange(0)
    gradients(0)
    up_first(rt.at[0], r2.at[0], zfirst[0], flow_up[0])
    up_first(rt.at[1], r2.at[1], zfirst[1], flow_up[1])
    forward_relay(2)
    up_second(r2.at[0], gg[0], zfirst[0], flow_up[0])
    down_done(r1.at[2], f.at[2], zfirst[2], flow_down[2])
    down_done(r1.at[3], f.at[3], zfirst[3], flow_down[3])
    scores(1)
    exchange(1)
    gradients(1)
    up_first(rt.at[2], r2.at[2], zfirst[2], flow_up[2])
    up_first(rt.at[3], r2.at[3], zfirst[3], flow_up[3])
    up_second(r2.at[1], gg[1], zfirst[1], flow_up[1])
    up_second(r2.at[2], gg[2], zfirst[2], flow_up[2])
    up_done(r2.at[0], gg[0], zfirst[0], flow_up[0])
    up_done(r2.at[1], gg[1], zfirst[1], flow_up[1])
    finish(0)
    up_second(r2.at[3], gg[3], zfirst[3], flow_up[3])
    up_done(r2.at[2], gg[2], zfirst[2], flow_up[2])
    up_done(r2.at[3], gg[3], zfirst[3], flow_up[3])
    finish(1)

    for h in range(heads):
        drain(pk.at[h], zfirst[h], flow_down[h], True)
        drain(pk.at[h], zfirst[h], flow_up[h], False)
    for stage in range(heads // 2):
        drain(ws.at[stage], True, flow_stat[stage], True)
        drain(ws.at[stage], True, flow_stat[stage] + 2, False)
    for n, (src, dst) in enumerate(inputs):
        head_wait(dst, ssem.at[flow_head + n])


def local(mesh_seq, mesh_head, queries, keys, values, dout, selected):
    zn, hn = ZN, mesh_head
    xn = mesh_seq // zn
    rows, features = queries.shape
    heads = features // hn // HD
    tokens = rows * hn
    blocks = tokens // QB
    far = zn * QB
    width = heads * HD
    own = lax.axis_index("seq")
    slot = jnp.arange(mesh_seq, dtype=jnp.int32)
    hit = (selected[None] == slot[:, None, None]) & (selected[None] != own)
    hit = jnp.any(hit, axis=2)
    inv = jnp.sum(jnp.where(hit, jnp.arange(blocks, dtype=jnp.int32)[None], 0), axis=1)
    flag = jnp.sum(hit.astype(jnp.int32), axis=1)
    lane = np.arange(far)
    spread = jnp.asarray((np.arange(HD)[:, None] == lane[None] % QB).astype(np.float32), BF)
    owner_mask = jnp.asarray((np.arange(zn)[:, None] == lane[None] // QB).astype(np.float32))
    flows = 4 * heads + 4 * (heads // 2) + 4
    block = lambda groups: pltpu.VMEM((heads, groups, zn, 2 * QB, HD), BF)
    stat = lambda groups: pltpu.VMEM((heads // 2, groups, zn, 1, HD), F32)
    shape = jax.ShapeDtypeStruct((tokens, width), BF)
    smem = pl.BlockSpec(memory_space=pltpu.SMEM)
    vmem = pl.BlockSpec(memory_space=pltpu.VMEM)
    hbm = pl.BlockSpec(memory_space=pl.ANY)
    scratch = (
        [pltpu.VMEM((tokens, width), BF)] * 4
        + [pltpu.VMEM((blocks, QB, width), F32)] * 2
        + [pltpu.VMEM((heads, tokens, HD), BF)] * 2
        + [pltpu.VMEM((heads, HD, tokens), BF)] * 2
        + [block(xn), block(xn), block(xn + 1), block(xn + 1), block(xn)]
        + [pltpu.VMEM((xn, zn, 2 * QB, HD), BF)] * heads
        + [stat(xn + 1), stat(xn)]
        + [pltpu.VMEM((xn, zn, 1, HD), F32)] * (heads // 2)
        + [stat(xn), stat(xn), stat(xn + 1)]
        + [pltpu.VMEM((2, xn + 1, far, HD), BF)] * 2
        + [pltpu.VMEM((2, xn + 1, tokens, far), F32)] * 2
        + [pltpu.VMEM((2, xn + 1, 1, far), F32)]
        + [pltpu.VMEM((xn + 1, 4, 1, far), F32)] * 2
        + [pltpu.VMEM((heads, tokens, HD), F32)] * 2
        + [pltpu.VMEM((TOPK + 1, zn, HD), F32)]
        + [pltpu.VMEM((zn, 1, HD), F32)] * 2
        + [pltpu.VMEM((zn, 2 * QB, HD), F32)]
        + [pltpu.SemaphoreType.DMA((flows, zn))] * 2
        + [pltpu.SemaphoreType.DMA((4,))]
    )
    return pl.pallas_call(
        functools.partial(kernel, xn, zn, hn, heads),
        out_shape=(shape,) * 4,
        in_specs=[smem] * 3 + [vmem] * 2 + [hbm] * 4,
        out_specs=(vmem,) * 4,
        scratch_shapes=scratch,
        compiler_params=pltpu.CompilerParams(
            collective_id=0, has_side_effects=True, vmem_limit_bytes=VMEM_LIMIT
        ),
    )(selected, inv, flag, spread, owner_mask, queries, keys, values, dout)


def solution(mesh):
    tokens = P(("seq", "head"), None)
    out = P("seq", "head")
    return jax.shard_map(
        functools.partial(local, mesh.shape["seq"], mesh.shape["head"]),
        mesh=mesh,
        in_specs=(tokens,) * 4 + (P("seq", None),),
        out_specs=(out,) * 4,
        check_vma=False,
    )
```

```python
import functools
import math

import jax
import jax.numpy as jnp
import numpy as np
from jax import lax
from jax.experimental import pallas as pl
from jax.experimental.pallas import tpu as pltpu
from jax.sharding import PartitionSpec as P

HD = 128
QB = 24
TOPK = 3
ZN = 16
NEGATIVE = -1e30
MESH = pl.DeviceIdType.MESH
BF = jnp.bfloat16
F32 = jnp.float32
VMEM_LIMIT = 60 * 1024 * 1024


def dot(a, b, ca, cb):
    return lax.dot_general(a, b, (((ca,), (cb,)), ((), ())), preferred_element_type=F32)


def split3(a):
    high = a.astype(BF)
    rest = a - high.astype(F32)
    mid = rest.astype(BF)
    low = (rest - mid.astype(F32)).astype(BF)
    return jnp.concatenate([high, mid, low], axis=0)


def loop(start, stop, body):
    def step(index, carry):
        body(index)
        return carry

    lax.fori_loop(start, stop, step, 0)


def kernel(
    xn, zn, hn, heads,
    sel, inv, flag, spread, owner_mask, q_in, k_in, v_in, g_in,
    att, gq, gk, gv,
    qa, ka, va, ga, qf, gf, kh, vh, kt, vt,
    pk, r1, f, rt, r2, gg, su, srx, sr, ws, wrz, wr,
    qc, gc, pb, db, li, sv, wv, dk, dv, aj, lr, dr, fo,
    ssem, rsem, lsem,
):
    scale = 1.0 / math.sqrt(HD)
    seq = lax.axis_index("seq")
    head = lax.axis_index("head")
    x = lax.div(seq, zn)
    z = lax.rem(seq, zn)
    rows = q_in.shape[0]
    width = heads * HD
    tokens = qa.shape[0]
    far = zn * QB

    def z_partner(k):
        half = lax.div(k + 1, 2)
        return lax.rem(z + jnp.where(lax.rem(k, 2) == 1, half, zn - half), zn)

    def when(value, most, body):
        for m in range(1, most + 1):
            pl.when(value == m)(functools.partial(body, m))

    def wait(part, sem):
        pltpu.make_async_copy(part, part, sem).wait()

    def z_send(src, dst, lower, flow):
        start = 0 if lower else x + 1

        def send(m):
            def body(k):
                zi = z_partner(k)
                pltpu.make_async_remote_copy(
                    src_ref=src.at[pl.ds(start, m), zi],
                    dst_ref=dst.at[pl.ds(start, m), z],
                    send_sem=ssem.at[flow],
                    recv_sem=rsem.at[flow],
                    device_id={"seq": x * zn + zi},
                    device_id_type=MESH,
                ).start()

            loop(1, zn, body)

        when(x if lower else xn - 1 - x, xn - 1, send)

    def z_wait(buf, lower, sem):
        full = lambda m: wait(buf.at[pl.ds(0, m), pl.ds(0, zn - 1)], sem)
        when(x if lower else xn - 1 - x, xn - 1, full)

    def x_send(src, dst, down, flow):
        def body(xi):
            pltpu.make_async_remote_copy(
                src_ref=src.at[xi],
                dst_ref=dst.at[x],
                send_sem=ssem.at[flow],
                recv_sem=rsem.at[flow],
                device_id={"seq": xi * zn + z},
                device_id_type=MESH,
            ).start()

        if down:
            loop(0, x, body)
        else:
            loop(x + 1, xn, body)

    def x_wait(buf, down, sem, sent):
        full = lambda m: wait(buf.at[pl.ds(0, m)], sem)
        when(x if down == sent else xn - 1 - x, xn - 1, full)

    def near_send(src, dst, down, flow):
        def body(zi):
            pltpu.make_async_remote_copy(
                src_ref=src(zi),
                dst_ref=dst(z),
                send_sem=ssem.at[flow],
                recv_sem=rsem.at[flow],
                device_id={"seq": x * zn + zi},
                device_id_type=MESH,
            ).start()

        if down:
            loop(0, z, body)
        else:
            loop(z + 1, zn, body)

    def near_wait(part, down, sem, sent):
        when(z if down == sent else zn - 1 - z, zn - 1, lambda m: wait(part(m), sem))

    def bulk_at(ref):
        return lambda zi: ref.at[:, x, zi]

    def stat_at(ref):
        return lambda zi: ref.at[x, zi]

    def bulk_part(m):
        return pk.at[:, 0, pl.ds(0, m)]

    def stat_part(m):
        return ws.at[0, pl.ds(0, m)]

    def keep(dst, src, index):
        dst[index] = src[index]

    def down_first(src, mid, zf, flow):
        if zf:
            loop(0, x, lambda i: keep(mid, src, (i, z)))
            z_send(src, mid, True, flow)
        else:
            x_send(src, mid, True, flow)

    def down_second(mid, dst, zf, flow):
        if zf:
            z_wait(mid, True, rsem.at[flow])
            x_send(mid, dst, True, flow + 1)
        else:
            x_wait(mid, True, rsem.at[flow], False)
            z_send(mid, dst, False, flow + 1)

    def down_done(mid, dst, zf, flow):
        if zf:
            x_wait(dst, True, rsem.at[flow + 1], False)
        else:
            loop(x + 1, xn, lambda i: keep(dst, mid, (i, z)))
            z_wait(dst, False, rsem.at[flow + 1])

    def up_first(src, mid, zf, flow):
        if zf:
            x_send(src, mid, False, flow)
        else:
            loop(x + 1, xn, lambda i: keep(mid, src, (i, z)))
            z_send(src, mid, False, flow)

    def up_second(mid, dst, zf, flow):
        if zf:
            x_wait(mid, False, rsem.at[flow], False)
            z_send(mid, dst, True, flow + 1)
        else:
            z_wait(mid, False, rsem.at[flow])
            x_send(mid, dst, False, flow + 1)

    def up_done(mid, dst, zf, flow):
        if zf:
            loop(0, x, lambda i: keep(dst, mid, (i, z)))
            z_wait(dst, True, rsem.at[flow + 1])
        else:
            x_wait(dst, False, rsem.at[flow + 1], False)

    def drain(buf, zf, flow, down):
        first_z = zf if down else not zf
        z_flow = flow if first_z else flow + 1
        x_flow = flow + 1 if first_z else flow
        z_wait(buf, zf, ssem.at[z_flow])
        x_wait(buf, down, ssem.at[x_flow], True)

    zfirst = [h % 2 == 0 for h in range(heads)]
    flow_down = [4 * h for h in range(heads)]
    flow_up = [4 * h + 2 for h in range(heads)]
    flow_stat = 4 * heads
    flow_head = 4 * heads + 4
    flow_near = 4 * heads + 8

    def drain_heads():
        for n in range(4):
            head_wait(inputs[n][1], ssem.at[flow_head + n])

    f[...] = jnp.zeros_like(f)
    wr[...] = jnp.zeros_like(wr)
    sr[...] = jnp.zeros_like(sr)

    barrier = pltpu.get_barrier_semaphore()

    def greet(target):
        pl.semaphore_signal(barrier, inc=1, device_id=target, device_id_type=MESH)

    loop(1, hn, lambda i: greet({"head": lax.rem(head + i, hn)}))
    loop(1, zn, lambda i: greet({"seq": x * zn + lax.rem(z + i, zn)}))
    loop(1, xn, lambda i: greet({"seq": lax.rem(x + i, xn) * zn + z}))
    pl.semaphore_wait(barrier, hn + zn + xn - 3)

    inputs = ((q_in, qa), (g_in, ga), (k_in, ka), (v_in, va))
    here = pl.ds(pl.multiple_of(head * rows, rows), rows)

    def spread_heads(n):
        src, dst = inputs[n]

        def fan(i):
            hi = lax.rem(head + i, hn)
            pltpu.make_async_remote_copy(
                src_ref=src.at[:, pl.ds(pl.multiple_of(hi * width, width), width)],
                dst_ref=dst.at[here],
                send_sem=ssem.at[flow_head + n],
                recv_sem=rsem.at[flow_head + n],
                device_id={"head": hi},
                device_id_type=MESH,
            ).start()

        loop(1, hn, fan)
        pltpu.make_async_copy(
            src.at[:, pl.ds(pl.multiple_of(head * width, width), width)], dst.at[here], lsem.at[n]
        ).start()

    def head_wait(dst, sem):
        if hn > 1:
            wait(dst.at[pl.ds(0, (hn - 1) * rows)], sem)

    def arrive(n):
        src, dst = inputs[n]
        pltpu.make_async_copy(
            src.at[:, pl.ds(pl.multiple_of(head * width, width), width)], dst.at[here], lsem.at[n]
        ).wait()
        head_wait(dst, rsem.at[flow_head + n])

    spread_heads(0)
    spread_heads(1)
    arrive(0)
    qf[...] = qa[...].astype(F32).reshape(qf.shape)
    arrive(1)
    gf[...] = ga[...].astype(F32).reshape(gf.shape)
    spread_heads(2)
    spread_heads(3)

    def block_of(i, h):
        cols = slice(h * HD, (h + 1) * HD)
        return jnp.concatenate([qf[i, :, cols], gf[i, :, cols]], axis=0).astype(BF)

    def pack(stage):
        def body(zd):
            for h in (2 * stage, 2 * stage + 1):
                f[h, xn, zd] = block_of(zd, h)
            for xd in range(xn):
                i = inv[xd * zn + zd]
                for h in (2 * stage, 2 * stage + 1):
                    pk[h, xd, zd] = block_of(i, h)

        loop(0, zn, body)

    def start_down(h):
        down_first(pk.at[h], r1.at[h], zfirst[h], flow_down[h])

    def forward_relay(h):
        down_second(r1.at[h], f.at[h], zfirst[h], flow_down[h])

    def arrived(h):
        down_done(r1.at[h], f.at[h], zfirst[h], flow_down[h])

    def start_up(h):
        up_first(rt.at[h], r2.at[h], zfirst[h], flow_up[h])

    def return_relay(h):
        up_second(r2.at[h], gg.at[h], zfirst[h], flow_up[h])

    def returned(h):
        up_done(r2.at[h], gg.at[h], zfirst[h], flow_up[h])

    def scores(h, first, last):
        u = lax.broadcasted_iota(jnp.int32, (tokens, far), 0)
        t = lax.broadcasted_iota(jnp.int32, (tokens, far), 1)

        def body(group):
            both = f[h, group].astype(F32)
            qv = both[:, :QB].reshape(far, HD).astype(BF)
            gv_ = both[:, QB:].reshape(far, HD).astype(BF)
            qc[h, group] = qv
            gc[h, group] = gv_
            s = dot(kh[h], qv, 1, 1)
            dp = dot(vh[h], gv_, 1, 1)
            s = jnp.where(u <= t + jnp.where(group == xn, 0, tokens), s, NEGATIVE)
            peak = jnp.max(s, axis=0, keepdims=True)
            p = jnp.exp((s - peak) * scale)
            total = jnp.sum(p, axis=0, keepdims=True)
            pb[h, group] = p
            db[h, group] = dp
            inverse = 1.0 / total
            li[h, group] = inverse
            sv[group, h] = peak * scale + jnp.log(total)
            sv[group, heads + h] = jnp.sum(p * dp, axis=0, keepdims=True) * inverse

        loop(first, last, body)

    def statistics(stage):
        picks = (2 * stage, 2 * stage + 1, heads + 2 * stage, heads + 2 * stage + 1)

        def to_rows(group):
            mask = owner_mask[...]
            parts = split3(jnp.concatenate([sv[group, k] * mask for k in picks], axis=0))
            flat = dot(parts, spread[...], 1, 1)
            flat = flat[: 4 * zn] + flat[4 * zn : 8 * zn] + flat[8 * zn :]
            out = flat[:zn]
            for k in range(1, 4):
                out = out + pltpu.roll(flat[k * zn : (k + 1) * zn], QB * k, 1)
            for i in range(zn):
                su[group, i, pl.ds(stage, 1)] = out[i : i + 1]

        loop(x, xn + 1, to_rows)

    def combine(stage):
        lane = lax.broadcasted_iota(jnp.int32, (1, HD), 1)

        def gather(i):
            aj[0, pl.ds(i, 1)] = su[xn, i, pl.ds(stage, 1)]
            for j in range(TOPK):
                c = sel[i, j]
                row = sr[lax.div(c, zn), lax.rem(c, zn), pl.ds(stage, 1)]
                aj[1 + j, pl.ds(i, 1)] = jnp.where(c == seq, NEGATIVE, row)

        loop(0, zn, gather)
        every = [aj[j] for j in range(TOPK + 1)]
        peak = functools.reduce(jnp.maximum, every)
        total = functools.reduce(jnp.add, [jnp.exp(a - peak) for a in every])
        lse = peak + jnp.log(total)
        weights = [jnp.exp(a - lse) for a in every]
        delta = functools.reduce(
            jnp.add, [pltpu.roll(w, 2 * QB, 1) * a for w, a in zip(weights, every)]
        )
        own = jnp.where(lane < 2 * QB, weights[0], delta)
        for i in range(zn):
            wr[xn, i, pl.ds(stage, 1)] = own[i : i + 1]
            lr[i] = lse[i : i + 1]
            dr[i] = delta[i : i + 1]

        def slots(xd):
            for zd in range(zn):
                c = xd * zn + zd
                i = inv[c]
                line = jnp.where(flag[c] > 0, lr[i], -NEGATIVE)
                w = jnp.exp(sr[xd, zd, pl.ds(stage, 1)] - line)
                ws[xd, zd, pl.ds(stage, 1)] = jnp.where(lane < 2 * QB, w, dr[i])

        loop(0, xn, slots)

    def weights_of(stage):
        def to_lanes(group):
            m = jnp.concatenate([wr[group, i, pl.ds(stage, 1)] for i in range(zn)], axis=0)
            wide = [m] + [pltpu.roll(m, HD - QB * k, 1) for k in range(1, 4)]
            flat = dot(split3(jnp.concatenate(wide, axis=0)), spread[...], 1, 0)
            flat = flat[: 4 * zn] + flat[4 * zn : 8 * zn] + flat[8 * zn :]
            mask = owner_mask[...]
            for k, pick in enumerate((2 * stage, 2 * stage + 1, heads + 2 * stage, heads + 2 * stage + 1)):
                wv[group, pick] = jnp.sum(flat[k * zn : (k + 1) * zn] * mask, axis=0, keepdims=True)

        loop(x, xn + 1, to_lanes)

    def gradients(h, first, last):
        def body(group):
            p = pb[h, group] * (wv[group, h] * li[h, group])
            pr = p.astype(BF)
            ds = (p * (db[h, group] - wv[group, heads + h])).astype(BF)
            out = dot(vt[h], pr, 1, 0).T.reshape(zn, QB, HD)
            dq = (dot(kt[h], ds, 1, 0) * scale).T.reshape(zn, QB, HD)
            rt[h, group] = jnp.concatenate([out, dq], axis=1).astype(BF)
            dk[h] += dot(ds, qc[h, group], 1, 0)
            dv[h] += dot(pr, gc[h, group], 1, 0)

        loop(first, last, body)

    def finish(h):
        def body(i):
            acc = rt[h, xn, i].astype(F32)
            for j in range(TOPK):
                c = sel[i, j]
                part = gg[h, lax.div(c, zn), lax.rem(c, zn)].astype(F32)
                acc = acc + jnp.where(c == seq, 0.0, part)
            fo[i] = acc

        loop(0, zn, body)
        cols = slice(h * HD, (h + 1) * HD)
        att[:, cols] = fo[:, :QB].reshape(tokens, HD).astype(BF)
        gq[:, cols] = fo[:, QB:].reshape(tokens, HD).astype(BF)

    def finish_keys(h):
        cols = slice(h * HD, (h + 1) * HD)
        gk[:, cols] = (dk[h] * scale).astype(BF)
        gv[:, cols] = dv[h].astype(BF)

    def key_heads():
        for h in range(heads):
            cols = slice(h * HD, (h + 1) * HD)
            kh[h] = ka[:, cols]
            vh[h] = va[:, cols]
            kt[h] = ka[:, cols].T
            vt[h] = va[:, cols].T
        dk[...] = jnp.zeros_like(dk)
        dv[...] = jnp.zeros_like(dv)

    near = flow_near
    pack(0)
    pack(1)
    start_down(1)
    start_down(3)
    pl.when(x < xn // 2)(lambda: near_send(bulk_at(pk), bulk_at(f), True, near))
    start_down(0)
    start_down(2)
    pl.when(x >= xn // 2)(lambda: near_send(bulk_at(pk), bulk_at(f), True, near))
    forward_relay(1)
    arrive(2)
    arrive(3)
    key_heads()
    forward_relay(3)
    forward_relay(0)
    arrived(0)
    scores(0, x + 1, xn + 1)
    arrived(1)
    scores(1, x + 1, xn + 1)
    forward_relay(2)
    near_wait(bulk_part, True, rsem.at[near], False)
    loop(0, heads, lambda h: scores(h, x, x + 1))
    statistics(0)
    arrived(2)
    scores(2, x + 1, xn + 1)
    arrived(3)
    scores(3, x + 1, xn + 1)
    statistics(1)
    up_first(su, srx, True, flow_stat + 2)
    near_send(stat_at(su), stat_at(sr), False, near + 3)
    up_second(srx, sr, True, flow_stat + 2)
    up_done(srx, sr, True, flow_stat + 2)
    near_wait(stat_part, False, rsem.at[near + 3], False)
    combine(0)
    combine(1)
    down_first(ws, wrz, True, flow_stat)
    near_send(stat_at(ws), stat_at(wr), True, near + 2)
    down_second(wrz, wr, True, flow_stat)
    down_done(wrz, wr, True, flow_stat)
    near_wait(stat_part, True, rsem.at[near + 2], False)
    weights_of(0)
    gradients(0, x + 1, xn + 1)
    start_up(0)
    gradients(1, x + 1, xn + 1)
    start_up(1)
    weights_of(1)
    loop(0, heads, lambda h: gradients(h, x, x + 1))
    pl.when(x >= xn // 2)(lambda: near_send(bulk_at(rt), bulk_at(gg), False, near + 1))
    gradients(2, x + 1, xn + 1)
    start_up(2)
    return_relay(0)
    gradients(3, x + 1, xn + 1)
    start_up(3)
    pl.when(x < xn // 2)(lambda: near_send(bulk_at(rt), bulk_at(gg), False, near + 1))
    return_relay(2)
    finish_keys(0)
    finish_keys(1)
    finish_keys(2)
    finish_keys(3)
    return_relay(1)
    return_relay(3)
    drain_heads()
    for h in range(heads):
        drain(pk.at[h], zfirst[h], flow_down[h], True)
    drain(ws, True, flow_stat, True)
    drain(ws, True, flow_stat + 2, False)
    near_wait(bulk_part, True, ssem.at[near], True)
    near_wait(stat_part, True, ssem.at[near + 2], True)
    near_wait(stat_part, False, ssem.at[near + 3], True)
    returned(0)
    returned(1)
    returned(2)
    returned(3)
    near_wait(bulk_part, False, rsem.at[near + 1], False)
    finish(0)
    finish(1)
    finish(2)
    finish(3)
    for h in range(heads):
        drain(pk.at[h], zfirst[h], flow_up[h], False)
    near_wait(bulk_part, False, ssem.at[near + 1], True)


def local(mesh_seq, mesh_head, queries, keys, values, dout, selected):
    zn, hn = ZN, mesh_head
    xn = mesh_seq // zn
    rows, features = queries.shape
    heads = features // hn // HD
    tokens = rows * hn
    blocks = tokens // QB
    far = zn * QB
    width = heads * HD
    own = lax.axis_index("seq")
    slot = jnp.arange(mesh_seq, dtype=jnp.int32)
    hit = (selected[None] == slot[:, None, None]) & (selected[None] != own)
    hit = jnp.any(hit, axis=2)
    inv = jnp.sum(jnp.where(hit, jnp.arange(blocks, dtype=jnp.int32)[None], 0), axis=1)
    flag = jnp.sum(hit.astype(jnp.int32), axis=1)
    lane = np.arange(far)
    spread = jnp.asarray((np.arange(HD)[:, None] == lane[None] % QB).astype(np.float32), BF)
    owner_mask = jnp.asarray((np.arange(zn)[:, None] == lane[None] // QB).astype(np.float32))
    flows = 4 * heads + 12
    block = lambda groups: pltpu.VMEM((heads, groups, zn, 2 * QB, HD), BF)
    stat = lambda groups: pltpu.VMEM((groups, zn, heads // 2, HD), F32)
    shape = jax.ShapeDtypeStruct((tokens, width), BF)
    smem = pl.BlockSpec(memory_space=pltpu.SMEM)
    vmem = pl.BlockSpec(memory_space=pltpu.VMEM)
    hbm = pl.BlockSpec(memory_space=pl.ANY)
    scratch = (
        [pltpu.VMEM((tokens, width), BF)] * 4
        + [pltpu.VMEM((blocks, QB, width), F32)] * 2
        + [pltpu.VMEM((heads, tokens, HD), BF)] * 2
        + [pltpu.VMEM((heads, HD, tokens), BF)] * 2
        + [block(xn), block(xn), block(xn + 1), block(xn + 1), block(xn), block(xn)]
        + [stat(xn + 1), stat(xn), stat(xn), stat(xn), stat(xn), stat(xn + 1)]
        + [pltpu.VMEM((heads, xn + 1, far, HD), BF)] * 2
        + [pltpu.VMEM((heads, xn + 1, tokens, far), F32)] * 2
        + [pltpu.VMEM((heads, xn + 1, 1, far), F32)]
        + [pltpu.VMEM((xn + 1, 2 * heads, 1, far), F32)] * 2
        + [pltpu.VMEM((heads, tokens, HD), F32)] * 2
        + [pltpu.VMEM((TOPK + 1, zn, HD), F32)]
        + [pltpu.VMEM((zn, 1, HD), F32)] * 2
        + [pltpu.VMEM((zn, 2 * QB, HD), F32)]
        + [pltpu.SemaphoreType.DMA((flows,))] * 2
        + [pltpu.SemaphoreType.DMA((4,))]
    )
    return pl.pallas_call(
        functools.partial(kernel, xn, zn, hn, heads),
        out_shape=(shape,) * 4,
        in_specs=[smem] * 3 + [vmem] * 2 + [hbm] * 4,
        out_specs=(vmem,) * 4,
        scratch_shapes=scratch,
        compiler_params=pltpu.CompilerParams(
            collective_id=0, has_side_effects=True, vmem_limit_bytes=VMEM_LIMIT
        ),
    )(selected, inv, flag, spread, owner_mask, queries, keys, values, dout)


def solution(mesh):
    tokens = P(("seq", "head"), None)
    out = P("seq", "head")
    return jax.shard_map(
        functools.partial(local, mesh.shape["seq"], mesh.shape["head"]),
        mesh=mesh,
        in_specs=(tokens,) * 4 + (P("seq", None),),
        out_specs=(out,) * 4,
        check_vma=False,
    )
```

```python
import functools
import math

import jax
import jax.numpy as jnp
import numpy as np
from jax import lax
from jax.experimental import pallas as pl
from jax.experimental.pallas import tpu as pltpu
from jax.sharding import PartitionSpec as P

HD = 128
QB = 24
TOPK = 3
ZN = 16
NEGATIVE = -1e30
MESH = pl.DeviceIdType.MESH
BF = jnp.bfloat16
F32 = jnp.float32
VMEM_LIMIT = 60 * 1024 * 1024


def dot(a, b, ca, cb):
    return lax.dot_general(a, b, (((ca,), (cb,)), ((), ())), preferred_element_type=F32)


def split3(a):
    high = a.astype(BF)
    rest = a - high.astype(F32)
    mid = rest.astype(BF)
    low = (rest - mid.astype(F32)).astype(BF)
    return jnp.concatenate([high, mid, low], axis=0)


def loop(start, stop, body):
    def step(index, carry):
        body(index)
        return carry

    lax.fori_loop(start, stop, step, 0)


def kernel(
    xn, zn, hn, heads,
    sel, inv, flag, spread, owner_mask, q_in, k_in, v_in, g_in,
    att, gq, gk, gv,
    qa, ka, va, ga, qf, gf, kh, vh, kt, vt,
    pk, r1, f, rt, r2, go, gd, su, srx, sr, ws, wrz, wr,
    qc, gc, pb, db, li, sv, wv, dk, dv, aj, lr, dr, fo, ob, wt,
    ssem, rsem, lsem,
):
    scale = 1.0 / math.sqrt(HD)
    seq = lax.axis_index("seq")
    head = lax.axis_index("head")
    x = lax.div(seq, zn)
    z = lax.rem(seq, zn)
    rows = q_in.shape[0]
    width = heads * HD
    tokens = qa.shape[0]
    far = zn * QB

    def z_partner(k):
        half = lax.div(k + 1, 2)
        return lax.rem(z + jnp.where(lax.rem(k, 2) == 1, half, zn - half), zn)

    def when(value, most, body):
        for m in range(1, most + 1):
            pl.when(value == m)(functools.partial(body, m))

    def wait(part, sem):
        pltpu.make_async_copy(part, part, sem).wait()

    def z_send(src, dst, lower, flow):
        start = 0 if lower else x + 1

        def send(m):
            def body(k):
                zi = z_partner(k)
                pltpu.make_async_remote_copy(
                    src_ref=src.at[pl.ds(start, m), zi],
                    dst_ref=dst.at[pl.ds(start, m), z],
                    send_sem=ssem.at[flow],
                    recv_sem=rsem.at[flow],
                    device_id={"seq": x * zn + zi},
                    device_id_type=MESH,
                ).start()

            loop(1, zn, body)

        when(x if lower else xn - 1 - x, xn - 1, send)

    def z_wait(buf, lower, sem):
        full = lambda m: wait(buf.at[pl.ds(0, m), pl.ds(0, zn - 1)], sem)
        when(x if lower else xn - 1 - x, xn - 1, full)

    def x_send(src, dst, down, flow):
        def body(xi):
            pltpu.make_async_remote_copy(
                src_ref=src.at[xi],
                dst_ref=dst.at[x],
                send_sem=ssem.at[flow],
                recv_sem=rsem.at[flow],
                device_id={"seq": xi * zn + z},
                device_id_type=MESH,
            ).start()

        if down:
            loop(0, x, body)
        else:
            loop(x + 1, xn, body)

    def x_wait(buf, down, sem, sent):
        full = lambda m: wait(buf.at[pl.ds(0, m)], sem)
        when(x if down == sent else xn - 1 - x, xn - 1, full)

    def near_send(src, dst, down, flow):
        def body(zi):
            pltpu.make_async_remote_copy(
                src_ref=src(zi),
                dst_ref=dst(z),
                send_sem=ssem.at[flow],
                recv_sem=rsem.at[flow],
                device_id={"seq": x * zn + zi},
                device_id_type=MESH,
            ).start()

        if down:
            loop(0, z, body)
        else:
            loop(z + 1, zn, body)

    def near_wait(part, down, sem, sent):
        when(z if down == sent else zn - 1 - z, zn - 1, lambda m: wait(part(m), sem))

    def bulk_at(ref):
        return lambda zi: ref.at[:, x, zi]

    def pair_at(ref, first):
        return lambda zi: ref.at[pl.ds(first, heads // 2), x, zi]

    def pair_part(m):
        return pk.at[pl.ds(0, heads // 2), 0, pl.ds(0, m)]

    def stat_at(ref):
        return lambda zi: ref.at[x, zi]

    def bulk_part(m):
        return pk.at[:, 0, pl.ds(0, m)]

    def stat_part(m):
        return ws.at[0, pl.ds(0, m)]

    def keep(dst, src, index):
        dst[index] = src[index]

    def down_first(src, mid, zf, flow):
        if zf:
            loop(0, x, lambda i: keep(mid, src, (i, z)))
            z_send(src, mid, True, flow)
        else:
            x_send(src, mid, True, flow)

    def down_second(mid, dst, zf, flow):
        if zf:
            z_wait(mid, True, rsem.at[flow])
            x_send(mid, dst, True, flow + 1)
        else:
            x_wait(mid, True, rsem.at[flow], False)
            z_send(mid, dst, False, flow + 1)

    def down_done(mid, dst, zf, flow):
        if zf:
            x_wait(dst, True, rsem.at[flow + 1], False)
        else:
            loop(x + 1, xn, lambda i: keep(dst, mid, (i, z)))
            z_wait(dst, False, rsem.at[flow + 1])

    def up_first(src, mid, zf, flow):
        if zf:
            x_send(src, mid, False, flow)
        else:
            loop(x + 1, xn, lambda i: keep(mid, src, (i, z)))
            z_send(src, mid, False, flow)

    def up_second(mid, dst, zf, flow):
        if zf:
            x_wait(mid, False, rsem.at[flow], False)
            z_send(mid, dst, True, flow + 1)
        else:
            z_wait(mid, False, rsem.at[flow])
            x_send(mid, dst, False, flow + 1)

    def up_done(mid, dst, zf, flow):
        if zf:
            loop(0, x, lambda i: keep(dst, mid, (i, z)))
            z_wait(dst, True, rsem.at[flow + 1])
        else:
            x_wait(dst, False, rsem.at[flow + 1], False)

    def drain(buf, zf, flow, down):
        first_z = zf if down else not zf
        z_flow = flow if first_z else flow + 1
        x_flow = flow + 1 if first_z else flow
        z_wait(buf, zf, ssem.at[z_flow])
        x_wait(buf, down, ssem.at[x_flow], True)

    zfirst = [h % 2 == 0 for h in range(heads)]
    flow_down = [4 * h for h in range(heads)]
    flow_up = [4 * h + 2 for h in range(heads)]
    flow_stat = 4 * heads
    flow_head = 4 * heads + 4
    flow_near = 4 * heads + 10

    def drain_heads():
        for n in range(6):
            head_wait(n, ssem.at[flow_head + n])

    f[...] = jnp.zeros_like(f)
    wr[...] = jnp.zeros_like(wr)
    sr[...] = jnp.zeros_like(sr)

    barrier = pltpu.get_barrier_semaphore()

    def greet(target):
        pl.semaphore_signal(barrier, inc=1, device_id=target, device_id_type=MESH)

    loop(1, hn, lambda i: greet({"head": lax.rem(head + i, hn)}))
    loop(1, zn, lambda i: greet({"seq": x * zn + lax.rem(z + i, zn)}))
    loop(1, xn, lambda i: greet({"seq": lax.rem(x + i, xn) * zn + z}))
    pl.semaphore_wait(barrier, hn + zn + xn - 3)

    half = width // 2
    inputs = (
        (q_in, qa, 0, half), (g_in, ga, 0, half), (q_in, qa, half, half), (g_in, ga, half, half),
        (k_in, ka, 0, width), (v_in, va, 0, width),
    )
    here = pl.ds(pl.multiple_of(head * rows, rows), rows)

    def columns(device, first, count):
        return pl.ds(pl.multiple_of(device * width + first, half), count)

    def spread_heads(n):
        src, dst, first, count = inputs[n]

        def fan(i):
            hi = lax.rem(head + i, hn)
            pltpu.make_async_remote_copy(
                src_ref=src.at[:, columns(hi, first, count)],
                dst_ref=dst.at[here, pl.ds(first, count)],
                send_sem=ssem.at[flow_head + n],
                recv_sem=rsem.at[flow_head + n],
                device_id={"head": hi},
                device_id_type=MESH,
            ).start()

        loop(1, hn, fan)
        pltpu.make_async_copy(
            src.at[:, columns(head, first, count)], dst.at[here, pl.ds(first, count)], lsem.at[n]
        ).start()

    def head_wait(n, sem):
        src, dst, first, count = inputs[n]
        if hn > 1:
            wait(dst.at[pl.ds(0, (hn - 1) * rows), pl.ds(first, count)], sem)

    def arrive(n):
        src, dst, first, count = inputs[n]
        pltpu.make_async_copy(
            src.at[:, columns(head, first, count)], dst.at[here, pl.ds(first, count)], lsem.at[n]
        ).wait()
        head_wait(n, rsem.at[flow_head + n])

    def widen(dst, src, first):
        part = src[:, first : first + half].astype(F32)
        dst[:, :, first : first + half] = part.reshape(tokens // QB, QB, half)

    def arrive_half(k):
        arrive(2 * k)
        widen(qf, qa, k * half)
        arrive(2 * k + 1)
        widen(gf, ga, k * half)

    for n in range(6):
        spread_heads(n)

    def block_of(i, h):
        cols = slice(h * HD, (h + 1) * HD)
        return jnp.concatenate([qf[i, :, cols], gf[i, :, cols]], axis=0).astype(BF)

    def pack(stage):
        def body(zd):
            for h in (2 * stage, 2 * stage + 1):
                f[h, xn, zd] = block_of(zd, h)
            for xd in range(xn):
                i = inv[xd * zn + zd]
                for h in (2 * stage, 2 * stage + 1):
                    pk[h, xd, zd] = block_of(i, h)

        loop(0, zn, body)

    back = [go.at[0], go.at[1], gd.at[0], gd.at[1]]

    def start_down(h):
        down_first(pk.at[h], r1.at[h], zfirst[h], flow_down[h])

    def forward_relay(h):
        down_second(r1.at[h], f.at[h], zfirst[h], flow_down[h])

    def arrived(h):
        down_done(r1.at[h], f.at[h], zfirst[h], flow_down[h])

    def start_up(h):
        up_first(rt.at[h], r2.at[h], zfirst[h], flow_up[h])

    def return_relay(h):
        up_second(r2.at[h], back[h], zfirst[h], flow_up[h])

    def returned(h):
        up_done(r2.at[h], back[h], zfirst[h], flow_up[h])

    def score_one(h, group):
        u = lax.broadcasted_iota(jnp.int32, (tokens, far), 0)
        t = lax.broadcasted_iota(jnp.int32, (tokens, far), 1)
        both = f[h, group].astype(F32)
        qv = both[:, :QB].reshape(far, HD).astype(BF)
        gv_ = both[:, QB:].reshape(far, HD).astype(BF)
        qc[h, group] = qv
        gc[h, group] = gv_
        s = dot(kh[h], qv, 1, 1)
        dp = dot(vh[h], gv_, 1, 1)
        s = jnp.where(u <= t + jnp.where(group == xn, 0, tokens), s, NEGATIVE)
        peak = jnp.max(s, axis=0, keepdims=True)
        p = jnp.exp((s - peak) * scale)
        total = jnp.sum(p, axis=0, keepdims=True)
        pb[h, group] = p
        db[h, group] = dp
        inverse = 1.0 / total
        li[h, group] = inverse
        sv[group, h] = peak * scale + jnp.log(total)
        sv[group, heads + h] = jnp.sum(p * dp, axis=0, keepdims=True) * inverse
        return (dot(vt[h], p.astype(BF), 1, 0) * inverse).T.reshape(zn, QB, HD)

    def scores(h):
        def body(group):
            out = score_one(h, group)
            if h % 2 == 0:
                ob[h // 2, group] = out
            else:
                rt[h // 2, group] = jnp.concatenate([ob[h // 2, group], out], axis=1).astype(BF)

        loop(x + 1, xn + 1, body)

    def near_scores():
        near_wait(bulk_part, True, rsem.at[near], False)

        def body(stage):
            both = [score_one(2 * stage, x), score_one(2 * stage + 1, x)]
            rt[stage, x] = jnp.concatenate(both, axis=1).astype(BF)

        loop(0, heads // 2, body)

    def statistics(stage, first, last):
        picks = (2 * stage, 2 * stage + 1, heads + 2 * stage, heads + 2 * stage + 1)

        def to_rows(group):
            mask = owner_mask[...]
            parts = split3(jnp.concatenate([sv[group, k] * mask for k in picks], axis=0))
            flat = dot(parts, spread[...], 1, 1)
            flat = flat[: 4 * zn] + flat[4 * zn : 8 * zn] + flat[8 * zn :]
            out = flat[:zn]
            for k in range(1, 4):
                out = out + pltpu.roll(flat[k * zn : (k + 1) * zn], QB * k, 1)
            for i in range(zn):
                su[group, i, pl.ds(stage, 1)] = out[i : i + 1]

        loop(first, last, to_rows)

    def combine(stage):
        lane = lax.broadcasted_iota(jnp.int32, (1, HD), 1)

        def gather(i):
            aj[0, pl.ds(i, 1)] = su[xn, i, pl.ds(stage, 1)]
            for j in range(TOPK):
                c = sel[i, j]
                row = sr[lax.div(c, zn), lax.rem(c, zn), pl.ds(stage, 1)]
                aj[1 + j, pl.ds(i, 1)] = jnp.where(c == seq, NEGATIVE, row)

        loop(0, zn, gather)
        every = [aj[j] for j in range(TOPK + 1)]
        peak = functools.reduce(jnp.maximum, every)
        total = functools.reduce(jnp.add, [jnp.exp(a - peak) for a in every])
        lse = peak + jnp.log(total)
        weights = [jnp.exp(a - lse) for a in every]
        delta = functools.reduce(
            jnp.add, [pltpu.roll(w, 2 * QB, 1) * a for w, a in zip(weights, every)]
        )
        own = jnp.where(lane < 2 * QB, weights[0], delta)
        for j in range(TOPK + 1):
            wt[stage, j] = weights[j].T
        for i in range(zn):
            wr[xn, i, pl.ds(stage, 1)] = own[i : i + 1]
            lr[i] = lse[i : i + 1]
            dr[i] = delta[i : i + 1]

        def slots(xd):
            for zd in range(zn):
                c = xd * zn + zd
                i = inv[c]
                line = jnp.where(flag[c] > 0, lr[i], -NEGATIVE)
                w = jnp.exp(sr[xd, zd, pl.ds(stage, 1)] - line)
                ws[xd, zd, pl.ds(stage, 1)] = jnp.where(lane < 2 * QB, w, dr[i])

        loop(0, xn, slots)

    def weights_of(stage):
        def to_lanes(group):
            m = jnp.concatenate([wr[group, i, pl.ds(stage, 1)] for i in range(zn)], axis=0)
            wide = [m] + [pltpu.roll(m, HD - QB * k, 1) for k in range(1, 4)]
            flat = dot(split3(jnp.concatenate(wide, axis=0)), spread[...], 1, 0)
            flat = flat[: 4 * zn] + flat[4 * zn : 8 * zn] + flat[8 * zn :]
            mask = owner_mask[...]
            for k, pick in enumerate((2 * stage, 2 * stage + 1, heads + 2 * stage, heads + 2 * stage + 1)):
                wv[group, pick] = jnp.sum(flat[k * zn : (k + 1) * zn] * mask, axis=0, keepdims=True)

        loop(x, xn + 1, to_lanes)

    def gradients(stage):
        def part(h, group):
            p = pb[h, group] * (wv[group, h] * li[h, group])
            pr = p.astype(BF)
            ds = (p * (db[h, group] - wv[group, heads + h])).astype(BF)
            dk[h] += dot(ds, qc[h, group], 1, 0)
            dv[h] += dot(pr, gc[h, group], 1, 0)
            return (dot(kt[h], ds, 1, 0) * scale).T.reshape(zn, QB, HD)

        def body(group):
            both = [part(2 * stage, group), part(2 * stage + 1, group)]
            rt[heads // 2 + stage, group] = jnp.concatenate(both, axis=1).astype(BF)

        loop(x, xn + 1, body)

    def unpack(dst, stage):
        for k in range(2):
            h = 2 * stage + k
            dst[:, h * HD : (h + 1) * HD] = fo[:, k * QB : (k + 1) * QB].reshape(tokens, HD).astype(BF)

    def finish_attended(stage):
        for i in range(zn):
            acc = wt[stage, 0, : 2 * QB, i : i + 1] * rt[stage, xn, i].astype(F32)
            for j in range(TOPK):
                c = sel[i, j]
                part = go[stage, lax.div(c, zn), lax.rem(c, zn)].astype(F32)
                part = wt[stage, 1 + j, : 2 * QB, i : i + 1] * part
                acc = acc + jnp.where(c == seq, 0.0, part)
            fo[i] = acc
        unpack(att, stage)

    def finish_queries(stage):
        def body(i):
            acc = rt[heads // 2 + stage, xn, i].astype(F32)
            for j in range(TOPK):
                c = sel[i, j]
                part = gd[stage, lax.div(c, zn), lax.rem(c, zn)].astype(F32)
                acc = acc + jnp.where(c == seq, 0.0, part)
            fo[i] = acc

        loop(0, zn, body)
        unpack(gq, stage)

    def finish_keys(h):
        cols = slice(h * HD, (h + 1) * HD)
        gk[:, cols] = (dk[h] * scale).astype(BF)
        gv[:, cols] = dv[h].astype(BF)

    def key_heads():
        for h in range(heads):
            cols = slice(h * HD, (h + 1) * HD)
            kh[h] = ka[:, cols]
            vh[h] = va[:, cols]
            kt[h] = ka[:, cols].T
            vt[h] = va[:, cols].T
        dk[...] = jnp.zeros_like(dk)
        dv[...] = jnp.zeros_like(dv)

    near = flow_near
    near_out, near_dq = near + 1, near + 4
    arrive_half(0)
    pack(0)
    start_down(1)
    start_down(0)
    arrive_half(1)
    pack(1)
    pl.when(x == 0)(lambda: near_send(bulk_at(pk), bulk_at(f), True, near))
    start_down(2)
    pl.when(x == xn - 1)(lambda: near_send(bulk_at(pk), bulk_at(f), True, near))
    forward_relay(1)
    x_wait(pk.at[1], True, ssem.at[flow_down[1]], True)
    start_down(3)
    arrive(4)
    arrive(5)
    key_heads()
    forward_relay(0)
    forward_relay(3)
    pl.when((x > 0) & (x < xn - 1))(lambda: near_send(bulk_at(pk), bulk_at(f), True, near))
    forward_relay(2)
    arrived(0)
    scores(0)
    arrived(1)
    scores(1)
    statistics(0, x + 1, xn + 1)
    pl.when(x == 0)(near_scores)
    arrived(2)
    scores(2)
    arrived(3)
    scores(3)
    statistics(1, x + 1, xn + 1)
    pl.when(x > 0)(near_scores)
    statistics(0, x, x + 1)
    statistics(1, x, x + 1)
    up_first(su, srx, True, flow_stat + 2)
    near_send(stat_at(su), stat_at(sr), False, near + 3)
    start_up(0)
    up_second(srx, sr, True, flow_stat + 2)
    near_send(pair_at(rt, 0), lambda zi: go.at[:, x, zi], False, near_out)
    up_done(srx, sr, True, flow_stat + 2)
    near_wait(stat_part, False, rsem.at[near + 3], False)
    combine(0)
    combine(1)
    down_first(ws, wrz, True, flow_stat)
    near_send(stat_at(ws), stat_at(wr), True, near + 2)
    start_up(1)
    return_relay(0)
    down_second(wrz, wr, True, flow_stat)
    down_done(wrz, wr, True, flow_stat)
    near_wait(stat_part, True, rsem.at[near + 2], False)
    weights_of(0)
    gradients(0)
    start_up(2)
    weights_of(1)
    gradients(1)
    start_up(3)
    near_send(pair_at(rt, 2), lambda zi: gd.at[:, x, zi], False, near_dq)
    return_relay(1)
    return_relay(2)
    for h in range(heads):
        finish_keys(h)
    returned(0)
    returned(1)
    near_wait(pair_part, False, rsem.at[near_out], False)
    finish_attended(0)
    finish_attended(1)
    return_relay(3)
    drain_heads()
    for h in range(heads):
        z_wait(pk.at[h], zfirst[h], ssem.at[flow_down[h] + 1 - zfirst[h]])
        if h != 1:
            x_wait(pk.at[h], True, ssem.at[flow_down[h] + zfirst[h]], True)
    drain(ws, True, flow_stat, True)
    drain(ws, True, flow_stat + 2, False)
    near_wait(bulk_part, True, ssem.at[near], True)
    near_wait(stat_part, True, ssem.at[near + 2], True)
    near_wait(stat_part, False, ssem.at[near + 3], True)
    near_wait(pair_part, False, ssem.at[near_out], True)
    returned(2)
    returned(3)
    near_wait(pair_part, False, rsem.at[near_dq], False)
    finish_queries(0)
    finish_queries(1)
    for h in range(heads):
        drain(pk.at[h], zfirst[h], flow_up[h], False)
    near_wait(pair_part, False, ssem.at[near_dq], True)


def local(mesh_seq, mesh_head, queries, keys, values, dout, selected):
    zn, hn = ZN, mesh_head
    xn = mesh_seq // zn
    rows, features = queries.shape
    heads = features // hn // HD
    tokens = rows * hn
    blocks = tokens // QB
    far = zn * QB
    width = heads * HD
    own = lax.axis_index("seq")
    slot = jnp.arange(mesh_seq, dtype=jnp.int32)
    hit = (selected[None] == slot[:, None, None]) & (selected[None] != own)
    hit = jnp.any(hit, axis=2)
    inv = jnp.sum(jnp.where(hit, jnp.arange(blocks, dtype=jnp.int32)[None], 0), axis=1)
    flag = jnp.sum(hit.astype(jnp.int32), axis=1)
    lane = np.arange(far)
    spread = jnp.asarray((np.arange(HD)[:, None] == lane[None] % QB).astype(np.float32), BF)
    owner_mask = jnp.asarray((np.arange(zn)[:, None] == lane[None] // QB).astype(np.float32))
    flows = 4 * heads + 15
    block = lambda groups: pltpu.VMEM((heads, groups, zn, 2 * QB, HD), BF)
    stat = lambda groups: pltpu.VMEM((groups, zn, heads // 2, HD), F32)
    shape = jax.ShapeDtypeStruct((tokens, width), BF)
    smem = pl.BlockSpec(memory_space=pltpu.SMEM)
    vmem = pl.BlockSpec(memory_space=pltpu.VMEM)
    hbm = pl.BlockSpec(memory_space=pl.ANY)
    scratch = (
        [pltpu.VMEM((tokens, width), BF)] * 4
        + [pltpu.VMEM((blocks, QB, width), F32)] * 2
        + [pltpu.VMEM((heads, tokens, HD), BF)] * 2
        + [pltpu.VMEM((heads, HD, tokens), BF)] * 2
        + [block(xn), block(xn), block(xn + 1), block(xn + 1), block(xn)]
        + [pltpu.VMEM((heads // 2, xn, zn, 2 * QB, HD), BF)] * 2
        + [stat(xn + 1), stat(xn), stat(xn), stat(xn), stat(xn), stat(xn + 1)]
        + [pltpu.VMEM((heads, xn + 1, far, HD), BF)] * 2
        + [pltpu.VMEM((heads, xn + 1, tokens, far), F32)] * 2
        + [pltpu.VMEM((heads, xn + 1, 1, far), F32)]
        + [pltpu.VMEM((xn + 1, 2 * heads, 1, far), F32)] * 2
        + [pltpu.VMEM((heads, tokens, HD), F32)] * 2
        + [pltpu.VMEM((TOPK + 1, zn, HD), F32)]
        + [pltpu.VMEM((zn, 1, HD), F32)] * 2
        + [pltpu.VMEM((zn, 2 * QB, HD), F32)]
        + [pltpu.VMEM((heads // 2, xn + 1, zn, QB, HD), F32)]
        + [pltpu.VMEM((heads // 2, TOPK + 1, HD, zn), F32)]
        + [pltpu.SemaphoreType.DMA((flows,))] * 2
        + [pltpu.SemaphoreType.DMA((6,))]
    )
    return pl.pallas_call(
        functools.partial(kernel, xn, zn, hn, heads),
        out_shape=(shape,) * 4,
        in_specs=[smem] * 3 + [vmem] * 2 + [hbm] * 4,
        out_specs=(vmem,) * 4,
        scratch_shapes=scratch,
        compiler_params=pltpu.CompilerParams(
            collective_id=0, has_side_effects=True, vmem_limit_bytes=VMEM_LIMIT
        ),
    )(selected, inv, flag, spread, owner_mask, queries, keys, values, dout)


def solution(mesh):
    tokens = P(("seq", "head"), None)
    out = P("seq", "head")
    return jax.shard_map(
        functools.partial(local, mesh.shape["seq"], mesh.shape["head"]),
        mesh=mesh,
        in_specs=(tokens,) * 4 + (P("seq", None),),
        out_specs=(out,) * 4,
        check_vma=False,
    )
```

```python
import functools
import math

import jax
import jax.numpy as jnp
import numpy as np
from jax import lax
from jax.experimental import pallas as pl
from jax.experimental.pallas import tpu as pltpu
from jax.sharding import PartitionSpec as P

HD = 128
QB = 24
TOPK = 3
ZN = 16
NEGATIVE = -1e30
MESH = pl.DeviceIdType.MESH
BF = jnp.bfloat16
F32 = jnp.float32
VMEM_LIMIT = 60 * 1024 * 1024


def dot(a, b, ca, cb):
    return lax.dot_general(a, b, (((ca,), (cb,)), ((), ())), preferred_element_type=F32)


def split3(a):
    high = a.astype(BF)
    rest = a - high.astype(F32)
    mid = rest.astype(BF)
    low = (rest - mid.astype(F32)).astype(BF)
    return jnp.concatenate([high, mid, low], axis=0)


def loop(start, stop, body):
    def step(index, carry):
        body(index)
        return carry

    lax.fori_loop(start, stop, step, 0)


def kernel(
    xn, zn, hn, heads,
    sel, inv, flag, spread, owner_mask, q_in, k_in, v_in, g_in,
    att, gq, gk, gv,
    qa, ka, va, ga, qf, gf, kh, vh, kt, vt,
    pk, r1, f, rt, r2, go, gd, su, srx, sr, ws, wrz, wr,
    qc, gc, pb, db, li, sv, wv, dk, dv, aj, lr, dr, fo, ob, wt,
    ssem, rsem, lsem,
):
    scale = 1.0 / math.sqrt(HD)
    seq = lax.axis_index("seq")
    head = lax.axis_index("head")
    x = lax.div(seq, zn)
    z = lax.rem(seq, zn)
    rows = q_in.shape[0]
    width = heads * HD
    tokens = qa.shape[0]
    far = zn * QB

    def z_partner(k):
        half = lax.div(k + 1, 2)
        return lax.rem(z + jnp.where(lax.rem(k, 2) == 1, half, zn - half), zn)

    def when(value, most, body):
        for m in range(1, most + 1):
            pl.when(value == m)(functools.partial(body, m))

    def wait(part, sem):
        pltpu.make_async_copy(part, part, sem).wait()

    def z_send(src, dst, lower, flow):
        start = 0 if lower else x + 1

        def send(m):
            def body(k):
                zi = z_partner(k)
                pltpu.make_async_remote_copy(
                    src_ref=src.at[pl.ds(start, m), zi],
                    dst_ref=dst.at[pl.ds(start, m), z],
                    send_sem=ssem.at[flow],
                    recv_sem=rsem.at[flow],
                    device_id={"seq": x * zn + zi},
                    device_id_type=MESH,
                ).start()

            loop(1, zn, body)

        when(x if lower else xn - 1 - x, xn - 1, send)

    def z_wait(buf, lower, sem):
        full = lambda m: wait(buf.at[pl.ds(0, m), pl.ds(0, zn - 1)], sem)
        when(x if lower else xn - 1 - x, xn - 1, full)

    def x_send(src, dst, down, flow):
        def body(xi):
            pltpu.make_async_remote_copy(
                src_ref=src.at[xi],
                dst_ref=dst.at[x],
                send_sem=ssem.at[flow],
                recv_sem=rsem.at[flow],
                device_id={"seq": xi * zn + z},
                device_id_type=MESH,
            ).start()

        if down:
            loop(0, x, body)
        else:
            loop(x + 1, xn, body)

    def x_wait(buf, down, sem, sent):
        full = lambda m: wait(buf.at[pl.ds(0, m)], sem)
        when(x if down == sent else xn - 1 - x, xn - 1, full)

    def near_send(src, dst, down, flow):
        def body(zi):
            pltpu.make_async_remote_copy(
                src_ref=src(zi),
                dst_ref=dst(z),
                send_sem=ssem.at[flow],
                recv_sem=rsem.at[flow],
                device_id={"seq": x * zn + zi},
                device_id_type=MESH,
            ).start()

        if down:
            loop(0, z, body)
        else:
            loop(0, zn - 1 - z, lambda i: body(zn - 1 - i))

    def near_wait(part, down, sem, sent):
        when(z if down == sent else zn - 1 - z, zn - 1, lambda m: wait(part(m), sem))

    def bulk_at(ref):
        return lambda zi: ref.at[:, x, zi]

    def pair_at(ref, first):
        return lambda zi: ref.at[pl.ds(first, heads // 2), x, zi]

    def pair_part(m):
        return pk.at[pl.ds(0, heads // 2), 0, pl.ds(0, m)]

    def stat_at(ref):
        return lambda zi: ref.at[x, zi]

    def bulk_part(m):
        return pk.at[:, 0, pl.ds(0, m)]

    def stat_part(m):
        return ws.at[0, pl.ds(0, m)]

    def keep(dst, src, index):
        dst[index] = src[index]

    def down_first(src, mid, zf, flow):
        if zf:
            loop(0, x, lambda i: keep(mid, src, (i, z)))
            z_send(src, mid, True, flow)
        else:
            x_send(src, mid, True, flow)

    def down_second(mid, dst, zf, flow):
        if zf:
            z_wait(mid, True, rsem.at[flow])
            x_send(mid, dst, True, flow + 1)
        else:
            x_wait(mid, True, rsem.at[flow], False)
            z_send(mid, dst, False, flow + 1)

    def down_done(mid, dst, zf, flow):
        if zf:
            x_wait(dst, True, rsem.at[flow + 1], False)
        else:
            loop(x + 1, xn, lambda i: keep(dst, mid, (i, z)))
            z_wait(dst, False, rsem.at[flow + 1])

    def up_first(src, mid, zf, flow):
        if zf:
            x_send(src, mid, False, flow)
        else:
            loop(x + 1, xn, lambda i: keep(mid, src, (i, z)))
            z_send(src, mid, False, flow)

    def up_second(mid, dst, zf, flow):
        if zf:
            x_wait(mid, False, rsem.at[flow], False)
            z_send(mid, dst, True, flow + 1)
        else:
            z_wait(mid, False, rsem.at[flow])
            x_send(mid, dst, False, flow + 1)

    def up_done(mid, dst, zf, flow):
        if zf:
            loop(0, x, lambda i: keep(dst, mid, (i, z)))
            z_wait(dst, True, rsem.at[flow + 1])
        else:
            x_wait(dst, False, rsem.at[flow + 1], False)

    def drain(buf, zf, flow, down):
        first_z = zf if down else not zf
        z_flow = flow if first_z else flow + 1
        x_flow = flow + 1 if first_z else flow
        z_wait(buf, zf, ssem.at[z_flow])
        x_wait(buf, down, ssem.at[x_flow], True)

    zfirst = [h % 2 == 0 for h in range(heads)]
    flow_down = [4 * h for h in range(heads)]
    flow_up = [4 * h + 2 for h in range(heads)]
    flow_stat = 4 * heads
    flow_head = 4 * heads + 4
    flow_near = 4 * heads + 10

    def drain_heads():
        for n in range(6):
            head_wait(n, ssem.at[flow_head + n])

    barrier = pltpu.get_barrier_semaphore()

    def greet(target):
        pl.semaphore_signal(barrier, inc=1, device_id=target, device_id_type=MESH)

    loop(1, hn, lambda i: greet({"head": lax.rem(head + i, hn)}))
    loop(1, zn, lambda i: greet({"seq": x * zn + lax.rem(z + i, zn)}))
    loop(1, xn, lambda i: greet({"seq": lax.rem(x + i, xn) * zn + z}))
    pl.semaphore_wait(barrier, hn + zn + xn - 3)

    half = width // 2
    inputs = (
        (q_in, qa, 0, half), (g_in, ga, 0, half), (q_in, qa, half, half), (g_in, ga, half, half),
        (k_in, ka, 0, width), (v_in, va, 0, width),
    )
    here = pl.ds(pl.multiple_of(head * rows, rows), rows)

    def columns(device, first, count):
        return pl.ds(pl.multiple_of(device * width + first, half), count)

    def spread_heads(n):
        src, dst, first, count = inputs[n]

        def fan(i):
            hi = lax.rem(head + i, hn)
            pltpu.make_async_remote_copy(
                src_ref=src.at[:, columns(hi, first, count)],
                dst_ref=dst.at[here, pl.ds(first, count)],
                send_sem=ssem.at[flow_head + n],
                recv_sem=rsem.at[flow_head + n],
                device_id={"head": hi},
                device_id_type=MESH,
            ).start()

        loop(1, hn, fan)
        pltpu.make_async_copy(
            src.at[:, columns(head, first, count)], dst.at[here, pl.ds(first, count)], lsem.at[n]
        ).start()

    def head_wait(n, sem):
        src, dst, first, count = inputs[n]
        if hn > 1:
            wait(dst.at[pl.ds(0, (hn - 1) * rows), pl.ds(first, count)], sem)

    def arrive(n):
        src, dst, first, count = inputs[n]
        pltpu.make_async_copy(
            src.at[:, columns(head, first, count)], dst.at[here, pl.ds(first, count)], lsem.at[n]
        ).wait()
        head_wait(n, rsem.at[flow_head + n])

    def widen(dst, src, first):
        part = src[:, first : first + half].astype(F32)
        dst[:, :, first : first + half] = part.reshape(tokens // QB, QB, half)

    def arrive_half(k):
        arrive(2 * k)
        widen(qf, qa, k * half)
        arrive(2 * k + 1)
        widen(gf, ga, k * half)

    for n in range(6):
        spread_heads(n)

    def clear(i):
        wr[x, i] = jnp.zeros((heads // 2, HD), F32)
        for h in range(heads):
            f[h, x, i] = jnp.zeros((2 * QB, HD), BF)

    loop(0, z + 1, clear)
    sr[x, z] = jnp.zeros((heads // 2, HD), F32)

    def block_of(i, h):
        cols = slice(h * HD, (h + 1) * HD)
        return jnp.concatenate([qf[i, :, cols], gf[i, :, cols]], axis=0).astype(BF)

    def pack(stage):
        def body(zd):
            for h in (2 * stage, 2 * stage + 1):
                f[h, xn, zd] = block_of(zd, h)
            for xd in range(xn):
                i = inv[xd * zn + zd]
                for h in (2 * stage, 2 * stage + 1):
                    pk[h, xd, zd] = block_of(i, h)

        loop(0, zn, body)

    back = [go.at[0], go.at[1], gd.at[0], gd.at[1]]

    def start_down(h):
        down_first(pk.at[h], r1.at[h], zfirst[h], flow_down[h])

    def forward_relay(h):
        down_second(r1.at[h], f.at[h], zfirst[h], flow_down[h])

    def arrived(h):
        down_done(r1.at[h], f.at[h], zfirst[h], flow_down[h])

    def start_up(h):
        up_first(rt.at[h], r2.at[h], zfirst[h], flow_up[h])

    def return_relay(h):
        up_second(r2.at[h], back[h], zfirst[h], flow_up[h])

    def returned(h):
        up_done(r2.at[h], back[h], zfirst[h], flow_up[h])

    def score_one(h, group):
        u = lax.broadcasted_iota(jnp.int32, (tokens, far), 0)
        t = lax.broadcasted_iota(jnp.int32, (tokens, far), 1)
        both = f[h, group].astype(F32)
        qv = both[:, :QB].reshape(far, HD).astype(BF)
        gv_ = both[:, QB:].reshape(far, HD).astype(BF)
        qc[h, group] = qv
        gc[h, group] = gv_
        s = dot(kh[h], qv, 1, 1)
        dp = dot(vh[h], gv_, 1, 1)
        s = jnp.where(u <= t + jnp.where(group == xn, 0, tokens), s, NEGATIVE)
        peak = jnp.max(s, axis=0, keepdims=True)
        p = jnp.exp((s - peak) * scale)
        total = jnp.sum(p, axis=0, keepdims=True)
        pb[h, group] = p
        db[h, group] = dp
        inverse = 1.0 / total
        li[h, group] = inverse
        sv[group, h] = peak * scale + jnp.log(total)
        sv[group, heads + h] = jnp.sum(p * dp, axis=0, keepdims=True) * inverse
        return (dot(vt[h], p.astype(BF), 1, 0) * inverse).T.reshape(zn, QB, HD)

    def scores(h):
        def body(group):
            out = score_one(h, group)
            if h % 2 == 0:
                ob[h // 2, group] = out
            else:
                rt[h // 2, group] = jnp.concatenate([ob[h // 2, group], out], axis=1).astype(BF)

        loop(x + 1, xn + 1, body)

    def near_scores():
        near_wait(bulk_part, True, rsem.at[near], False)

        def body(stage):
            both = [score_one(2 * stage, x), score_one(2 * stage + 1, x)]
            rt[stage, x] = jnp.concatenate(both, axis=1).astype(BF)

        loop(0, heads // 2, body)

    def picks_of(stage):
        return (2 * stage, 2 * stage + 1, heads + 2 * stage, heads + 2 * stage + 1)

    def statistics(stages, first, last):
        def to_rows(group):
            mask = owner_mask[...]
            for stage in stages:
                lines = [sv[group, k] * mask for k in picks_of(stage)]
                flat = dot(split3(jnp.concatenate(lines, axis=0)), spread[...], 1, 1)
                flat = flat[: 4 * zn] + flat[4 * zn : 8 * zn] + flat[8 * zn :]
                out = flat[:zn]
                for k in range(1, 4):
                    out = out + pltpu.roll(flat[k * zn : (k + 1) * zn], QB * k, 1)
                for i in range(zn):
                    su[group, i, pl.ds(stage, 1)] = out[i : i + 1]

        loop(first, last, to_rows)

    def combine(stage):
        lane = lax.broadcasted_iota(jnp.int32, (1, HD), 1)

        def gather(i):
            aj[0, pl.ds(i, 1)] = su[xn, i, pl.ds(stage, 1)]
            for j in range(TOPK):
                c = sel[i, j]
                row = sr[lax.div(c, zn), lax.rem(c, zn), pl.ds(stage, 1)]
                aj[1 + j, pl.ds(i, 1)] = jnp.where(c == seq, NEGATIVE, row)

        loop(0, zn, gather)
        every = [aj[j] for j in range(TOPK + 1)]
        peak = functools.reduce(jnp.maximum, every)
        total = functools.reduce(jnp.add, [jnp.exp(a - peak) for a in every])
        lse = peak + jnp.log(total)
        weights = [jnp.exp(a - lse) for a in every]
        delta = functools.reduce(
            jnp.add, [pltpu.roll(w, 2 * QB, 1) * a for w, a in zip(weights, every)]
        )
        own = jnp.where(lane < 2 * QB, weights[0], delta)
        for j in range(TOPK + 1):
            wt[stage, j] = weights[j].T
        for i in range(zn):
            wr[xn, i, pl.ds(stage, 1)] = own[i : i + 1]
            lr[i] = lse[i : i + 1]
            dr[i] = delta[i : i + 1]

        def slots(xd):
            for zd in range(zn):
                c = xd * zn + zd
                i = inv[c]
                line = jnp.where(flag[c] > 0, lr[i], -NEGATIVE)
                w = jnp.exp(sr[xd, zd, pl.ds(stage, 1)] - line)
                ws[xd, zd, pl.ds(stage, 1)] = jnp.where(lane < 2 * QB, w, dr[i])

        loop(0, xn, slots)

    def weights():
        def to_lanes(group):
            mask = owner_mask[...]
            for stage in range(heads // 2):
                m = jnp.concatenate([wr[group, i, pl.ds(stage, 1)] for i in range(zn)], axis=0)
                wide = [m] + [pltpu.roll(m, HD - QB * k, 1) for k in range(1, 4)]
                flat = dot(split3(jnp.concatenate(wide, axis=0)), spread[...], 1, 0)
                flat = flat[: 4 * zn] + flat[4 * zn : 8 * zn] + flat[8 * zn :]
                for k, pick in enumerate(picks_of(stage)):
                    part = flat[k * zn : (k + 1) * zn] * mask
                    wv[group, pick] = jnp.sum(part, axis=0, keepdims=True)

        loop(x, xn + 1, to_lanes)

    def gradients(stage):
        def part(h, group):
            p = pb[h, group] * (wv[group, h] * li[h, group])
            pr = p.astype(BF)
            ds = (p * (db[h, group] - wv[group, heads + h])).astype(BF)
            dk[h] += dot(ds, qc[h, group], 1, 0)
            dv[h] += dot(pr, gc[h, group], 1, 0)
            return (dot(kt[h], ds, 1, 0) * scale).T.reshape(zn, QB, HD)

        def body(group):
            both = [part(2 * stage, group), part(2 * stage + 1, group)]
            rt[heads // 2 + stage, group] = jnp.concatenate(both, axis=1).astype(BF)

        loop(x, xn + 1, body)

    def unpack(dst, stage):
        for k in range(2):
            h = 2 * stage + k
            dst[:, h * HD : (h + 1) * HD] = fo[:, k * QB : (k + 1) * QB].reshape(tokens, HD).astype(BF)

    def finish_attended(stage):
        for i in range(zn):
            acc = wt[stage, 0, : 2 * QB, i : i + 1] * rt[stage, xn, i].astype(F32)
            for j in range(TOPK):
                c = sel[i, j]
                part = go[stage, lax.div(c, zn), lax.rem(c, zn)].astype(F32)
                part = wt[stage, 1 + j, : 2 * QB, i : i + 1] * part
                acc = acc + jnp.where(c == seq, 0.0, part)
            fo[i] = acc
        unpack(att, stage)

    def finish_queries(stage):
        def body(i):
            acc = rt[heads // 2 + stage, xn, i].astype(F32)
            for j in range(TOPK):
                c = sel[i, j]
                part = gd[stage, lax.div(c, zn), lax.rem(c, zn)].astype(F32)
                acc = acc + jnp.where(c == seq, 0.0, part)
            fo[i] = acc

        loop(0, zn, body)
        unpack(gq, stage)

    def finish_keys(h):
        cols = slice(h * HD, (h + 1) * HD)
        gk[:, cols] = (dk[h] * scale).astype(BF)
        gv[:, cols] = dv[h].astype(BF)

    def key_heads():
        for h in range(heads):
            cols = slice(h * HD, (h + 1) * HD)
            kh[h] = ka[:, cols]
            vh[h] = va[:, cols]
            kt[h] = ka[:, cols].T
            vt[h] = va[:, cols].T
        dk[...] = jnp.zeros_like(dk)
        dv[...] = jnp.zeros_like(dv)

    near = flow_near
    near_out, near_dq = near + 1, near + 4
    arrive_half(0)
    pack(0)
    start_down(1)
    start_down(0)
    arrive_half(1)
    pack(1)
    pl.when(x == 0)(lambda: near_send(bulk_at(pk), bulk_at(f), True, near))
    start_down(2)
    pl.when(x == xn - 1)(lambda: near_send(bulk_at(pk), bulk_at(f), True, near))
    forward_relay(1)
    x_wait(pk.at[1], True, ssem.at[flow_down[1]], True)
    start_down(3)
    arrive(4)
    arrive(5)
    key_heads()
    forward_relay(0)
    forward_relay(3)
    pl.when((x > 0) & (x < xn - 1))(lambda: near_send(bulk_at(pk), bulk_at(f), True, near))
    forward_relay(2)
    arrived(0)
    scores(0)
    arrived(1)
    scores(1)
    statistics((0,), x + 1, xn + 1)
    pl.when(x == 0)(near_scores)
    arrived(2)
    scores(2)
    arrived(3)
    scores(3)
    statistics((1,), x + 1, xn + 1)
    pl.when(x > 0)(near_scores)
    statistics((0, 1), x, x + 1)
    up_first(su, srx, True, flow_stat + 2)
    near_send(stat_at(su), stat_at(sr), False, near + 3)
    start_up(0)
    up_second(srx, sr, True, flow_stat + 2)
    near_send(pair_at(rt, 0), lambda zi: go.at[:, x, zi], False, near_out)
    up_done(srx, sr, True, flow_stat + 2)
    near_wait(stat_part, False, rsem.at[near + 3], False)
    combine(0)
    combine(1)
    down_first(ws, wrz, True, flow_stat)
    near_send(stat_at(ws), stat_at(wr), True, near + 2)
    start_up(1)
    return_relay(0)
    down_second(wrz, wr, True, flow_stat)
    down_done(wrz, wr, True, flow_stat)
    near_wait(stat_part, True, rsem.at[near + 2], False)
    weights()
    gradients(1)
    start_up(3)
    gradients(0)
    start_up(2)
    near_send(pair_at(rt, 2), lambda zi: gd.at[:, x, zi], False, near_dq)
    return_relay(1)
    return_relay(2)
    for h in range(heads):
        finish_keys(h)
    returned(0)
    returned(1)
    near_wait(pair_part, False, rsem.at[near_out], False)
    finish_attended(0)
    finish_attended(1)
    return_relay(3)
    drain_heads()
    for h in range(heads):
        z_wait(pk.at[h], zfirst[h], ssem.at[flow_down[h] + 1 - zfirst[h]])
        if h != 1:
            x_wait(pk.at[h], True, ssem.at[flow_down[h] + zfirst[h]], True)
    drain(ws, True, flow_stat, True)
    drain(ws, True, flow_stat + 2, False)
    near_wait(bulk_part, True, ssem.at[near], True)
    near_wait(stat_part, True, ssem.at[near + 2], True)
    near_wait(stat_part, False, ssem.at[near + 3], True)
    near_wait(pair_part, False, ssem.at[near_out], True)
    returned(2)
    returned(3)
    near_wait(pair_part, False, rsem.at[near_dq], False)
    finish_queries(0)
    finish_queries(1)
    for h in range(heads):
        drain(pk.at[h], zfirst[h], flow_up[h], False)
    near_wait(pair_part, False, ssem.at[near_dq], True)


def settle(a, b, c, d, att, gq, gk, gv, held, sem):
    inward = [pltpu.make_async_copy(src, held.at[n], sem.at[n]) for n, src in enumerate((a, b, c, d))]
    outward = [
        pltpu.make_async_copy(held.at[n], dst, sem.at[4 + n]) for n, dst in enumerate((att, gq, gk, gv))
    ]
    for copy in inward:
        copy.start()
    for first, second in zip(inward, outward):
        first.wait()
        second.start()
    for copy in outward:
        copy.wait()


def local(mesh_seq, mesh_head, queries, keys, values, dout, selected):
    zn, hn = ZN, mesh_head
    xn = mesh_seq // zn
    rows, features = queries.shape
    heads = features // hn // HD
    tokens = rows * hn
    blocks = tokens // QB
    far = zn * QB
    width = heads * HD
    own = lax.axis_index("seq")
    slot = jnp.arange(mesh_seq, dtype=jnp.int32)
    hit = (selected[None] == slot[:, None, None]) & (selected[None] != own)
    hit = jnp.any(hit, axis=2)
    inv = jnp.sum(jnp.where(hit, jnp.arange(blocks, dtype=jnp.int32)[None], 0), axis=1)
    flag = jnp.sum(hit.astype(jnp.int32), axis=1)
    lane = np.arange(far)
    spread = jnp.asarray((np.arange(HD)[:, None] == lane[None] % QB).astype(np.float32), BF)
    owner_mask = jnp.asarray((np.arange(zn)[:, None] == lane[None] // QB).astype(np.float32))
    flows = 4 * heads + 15
    block = lambda groups: pltpu.VMEM((heads, groups, zn, 2 * QB, HD), BF)
    stat = lambda groups: pltpu.VMEM((groups, zn, heads // 2, HD), F32)
    shape = jax.ShapeDtypeStruct((tokens, width), BF)
    smem = pl.BlockSpec(memory_space=pltpu.SMEM)
    vmem = pl.BlockSpec(memory_space=pltpu.VMEM)
    hbm = pl.BlockSpec(memory_space=pl.ANY)
    scratch = (
        [pltpu.VMEM((tokens, width), BF)] * 4
        + [pltpu.VMEM((blocks, QB, width), F32)] * 2
        + [pltpu.VMEM((heads, tokens, HD), BF)] * 2
        + [pltpu.VMEM((heads, HD, tokens), BF)] * 2
        + [block(xn), block(xn), block(xn + 1), block(xn + 1), block(xn)]
        + [pltpu.VMEM((heads // 2, xn, zn, 2 * QB, HD), BF)] * 2
        + [stat(xn + 1), stat(xn), stat(xn), stat(xn), stat(xn), stat(xn + 1)]
        + [pltpu.VMEM((heads, xn + 1, far, HD), BF)] * 2
        + [pltpu.VMEM((heads, xn + 1, tokens, far), F32)] * 2
        + [pltpu.VMEM((heads, xn + 1, 1, far), F32)]
        + [pltpu.VMEM((xn + 1, 2 * heads, 1, far), F32)] * 2
        + [pltpu.VMEM((heads, tokens, HD), F32)] * 2
        + [pltpu.VMEM((TOPK + 1, zn, HD), F32)]
        + [pltpu.VMEM((zn, 1, HD), F32)] * 2
        + [pltpu.VMEM((zn, 2 * QB, HD), F32)]
        + [pltpu.VMEM((heads // 2, xn + 1, zn, QB, HD), F32)]
        + [pltpu.VMEM((heads // 2, TOPK + 1, HD, zn), F32)]
        + [pltpu.SemaphoreType.DMA((flows,))] * 2
        + [pltpu.SemaphoreType.DMA((6,))]
    )
    results = pl.pallas_call(
        functools.partial(kernel, xn, zn, hn, heads),
        out_shape=(shape,) * 4,
        in_specs=[smem] * 3 + [vmem] * 2 + [hbm] * 4,
        out_specs=(vmem,) * 4,
        scratch_shapes=scratch,
        compiler_params=pltpu.CompilerParams(
            collective_id=0, has_side_effects=True, vmem_limit_bytes=VMEM_LIMIT
        ),
    )(selected, inv, flag, spread, owner_mask, queries, keys, values, dout)
    return pl.pallas_call(
        settle,
        out_shape=(shape,) * 4,
        in_specs=[hbm] * 4,
        out_specs=(hbm,) * 4,
        scratch_shapes=[pltpu.VMEM((4, tokens, width), BF), pltpu.SemaphoreType.DMA((8,))],
        compiler_params=pltpu.CompilerParams(vmem_limit_bytes=VMEM_LIMIT),
    )(*results)


def solution(mesh):
    tokens = P(("seq", "head"), None)
    out = P("seq", "head")
    return jax.shard_map(
        functools.partial(local, mesh.shape["seq"], mesh.shape["head"]),
        mesh=mesh,
        in_specs=(tokens,) * 4 + (P("seq", None),),
        out_specs=(out,) * 4,
        check_vma=False,
    )
```
